128 devices in a mesh: ctx: 32 (over y, z, core), tp: 4 (over x).
Axes of the slice: x: 4, y: 4, z: 4, core: 2. Of those that a mesh axis runs over, the one named last changes fastest.
Arguments:
- tokens: bfloat16 [2, 2, 32, 64, 1024], P(None, None, 'ctx'), may hold values from -6 to 6
- norm_gain: float32 [1024], replicated, may hold values from 0.5 to 1.5
- query_weight: bfloat16 [1024, 1024], P(None, 'tp'), may hold values from -0.1875 to 0.1875
- key_weight: bfloat16 [1024, 512], P(None, 'tp'), may hold values from -0.1875 to 0.1875
- value_weight: bfloat16 [1024, 512], P(None, 'tp'), may hold values from -0.1875 to 0.1875
- query_gain: float32 [64], replicated, may hold values from 0.1 to 1.9
- key_gain: float32 [64], replicated, may hold values from 0.1 to 1.9
- out_weight: bfloat16 [1024, 1024], P('tp'), may hold values from -1.5 to 1.5
- post_gain: float32 [1024], replicated, may hold values from 0.5 to 1.5
- gate_weight: bfloat16 [1024, 4608], P(None, 'tp'), may hold values from -0.1875 to 0.1875
- up_weight: bfloat16 [1024, 4608], P(None, 'tp'), may hold values from -0.1875 to 0.1875
- down_weight: bfloat16 [4608, 1024], P('tp'), may hold values from -0.09375 to 0.09375
- cotangent: bfloat16 [2, 2, 32, 64, 1024], P(None, None, 'ctx'), may hold values from -6 to 6
Outputs:
- mixed: bfloat16 [2, 2, 32, 64, 1024], P(None, None, 'ctx')
- input_grad: bfloat16 [2, 2, 32, 64, 1024], P(None, None, 'ctx')
- norm_gain_grad: float32 [1024], replicated
- query_weight_grad: float32 [1024, 1024], P('ctx', 'tp')
- key_weight_grad: float32 [1024, 512], P('ctx', 'tp')
- value_weight_grad: float32 [1024, 512], P('ctx', 'tp')
- query_gain_grad: float32 [64], replicated
- key_gain_grad: float32 [64], replicated
- out_weight_grad: float32 [1024, 1024], P('tp', 'ctx')
- post_gain_grad: float32 [1024], replicated
- gate_weight_grad: float32 [1024, 4608], P('ctx', 'tp')
- up_weight_grad: float32 [1024, 4608], P('ctx', 'tp')
- down_weight_grad: float32 [4608, 1024], P('tp', 'ctx')
The draws below stay inside these ranges and needn't reach their ends.
All inputs are finite; a program needn't handle non-finite values.
Results may differ from the reference program's by a relative error of at most 0.025.
Values may be sent and summed in bfloat16 or wider, within the bound.
A program may use at most 128 MiB of HBM per device.

```python
import jax
import jax.numpy as jnp
from jax import lax

D = 1024
H = 16
KVH = 8
HD = 64
FF = 4608
SEQS = 2
BLK = 64
N_CTX = 32


def block_scale(key, extent, pieces, smallest, high):
    level, own = 1.0, jax.random.fold_in(key, 6)
    for axis_at, blocks in pieces:
        draws = jnp.exp(jax.random.uniform(jax.random.fold_in(own, axis_at), (blocks,), jnp.float32, smallest / len(pieces), high / len(pieces)))
        level = level * jnp.repeat(draws, extent[axis_at] // blocks).reshape([-1 if axis == axis_at else 1 for axis in range(len(extent))])
    return level


def noise(rng, extent, scale, reach, pieces=(), held_as=jnp.bfloat16):
    values = jax.random.normal(rng, extent, jnp.float32) * scale
    if len(pieces) > 0:
        values = block_scale(rng, extent, pieces, -0.22, 0.18) * values
    return jnp.clip(values, min=-reach, max=reach).astype(held_as)


def setup_inputs(seed: int = 0) -> dict:
    streams_of = jax.random.split(jax.random.key(seed), 14)
    tokens = noise(streams_of[0], (SEQS, 2, N_CTX, BLK, D), 1.0, 6.0, ((2, 32),))
    norm_gain = jnp.clip(1.0 + 0.1 * jax.random.normal(streams_of[1], (D,), jnp.float32), 0.5, 1.5)
    query_weight = noise(streams_of[2], (D, H * HD), D ** -0.5, 0.1875, ((1, 4),))
    key_weight = noise(streams_of[3], (D, KVH * HD), D ** -0.5, 0.1875, ((1, 4),))
    value_weight = noise(streams_of[4], (D, KVH * HD), D ** -0.5, 0.1875, ((1, 4),))
    query_gain = jnp.clip(1.0 + 0.18 * jax.random.normal(streams_of[5], (HD,), jnp.float32), 0.1, 1.9)
    key_gain = jnp.clip(1.0 + 0.18 * jax.random.normal(streams_of[6], (HD,), jnp.float32), 0.1, 1.9)
    out_weight = noise(streams_of[7], (H * HD, D), (H * HD // 64) ** -0.5, 1.5, ((0, 4),))
    post_gain = jnp.clip(1.0 + 0.1 * jax.random.normal(streams_of[8], (D,), jnp.float32), 0.5, 1.5)
    gate_weight = noise(streams_of[9], (D, FF), D ** -0.5, 0.1875, ((1, 4),))
    up_weight = noise(streams_of[10], (D, FF), D ** -0.5, 0.1875, ((1, 4),))
    down_weight = noise(streams_of[11], (FF, D), FF ** -0.5, 0.09375, ((0, 4),))
    cotangent = noise(streams_of[12], (SEQS, 2, N_CTX, BLK, D), 1.0, 6.0, ((2, 32),))
    return dict(tokens=tokens, norm_gain=norm_gain, query_weight=query_weight, key_weight=key_weight, value_weight=value_weight, query_gain=query_gain, key_gain=key_gain, out_weight=out_weight, post_gain=post_gain, gate_weight=gate_weight, up_weight=up_weight, down_weight=down_weight, cotangent=cotangent)


EPSILON = 1e-05
ROPE_BASE = 1000000.0
PRECISE = lax.Precision.HIGHEST

@jax.custom_vjp
def low(v):
    return lax.optimization_barrier(v.astype(jnp.bfloat16)).astype(jnp.float32)

@jax.custom_vjp
def low_back(v):
    return v

def low_keep(v):
    return (low(v), None)

def low_pass(kept, grad):
    return (grad,)

def back_keep(v):
    return (v, None)

def back_low(kept, grad):
    return (low(grad),)
low.defvjp(low_keep, low_pass)
low_back.defvjp(back_keep, back_low)

def rope_tables(positions, width):
    exponent = jnp.arange(0, width, 2).astype(jnp.float32) / width
    frequency = jnp.power(ROPE_BASE, -exponent)
    angles = positions.astype(jnp.float32)[:, None] * frequency[None, :]
    return (jnp.cos(angles), jnp.sin(angles))

def rotate(values, cosine, sine_part):
    middle = values.shape[-1] // 2
    leading = values[..., :middle]
    trailing = values[..., middle:]
    cos_rows = cosine[:, None, :]
    sin_rows = sine_part[:, None, :]
    return jnp.concatenate([leading * cos_rows - trailing * sin_rows, trailing * cos_rows + leading * sin_rows], -1)

def norm_rows(values, gain):
    return values * lax.rsqrt(lax.optimization_barrier(jnp.mean(values * values, -1, keepdims=True)) + EPSILON) * gain

def layer(inputs, norm_gain, query_weight, key_weight, value_weight, query_gain, key_gain, out_weight, post_gain, gate_weight, up_weight, down_weight):
    length = inputs.shape[0]
    score_scale = HD ** (-0.5)
    normed = low(norm_rows(inputs, norm_gain))
    queries = low_back(jnp.dot(normed, query_weight, precision=PRECISE)).reshape(length, H, HD)
    key_rows = low_back(jnp.dot(normed, key_weight, precision=PRECISE)).reshape(length, KVH, HD)
    value_rows = low(low_back(jnp.dot(normed, value_weight, precision=PRECISE))).reshape(length, KVH, HD)
    cosine, sine_part = rope_tables(jnp.arange(length), HD)
    queries = low(rotate(norm_rows(queries, query_gain), cosine, sine_part))
    key_rows = low(rotate(norm_rows(key_rows, key_gain), cosine, sine_part))
    block_rows = min(512, length)
    grouped = queries.reshape(length // block_rows, block_rows, KVH, H // KVH, HD)
    firsts = jnp.arange(length // block_rows) * block_rows
    key_places = jnp.arange(length)

    def attend(operand):
        q_block, first_row = operand
        scores = low_back(jnp.einsum('qkgd,skd->kgqs', q_block, key_rows, precision=PRECISE) * score_scale)
        visible = key_places[None, :] <= (first_row + jnp.arange(block_rows))[:, None]
        scores = jnp.where(visible, scores, -1e+30)
        row_max = lax.optimization_barrier(jnp.max(scores, -1, keepdims=True))
        unnormed = jnp.exp(scores - row_max)
        probability = low(unnormed / lax.optimization_barrier(jnp.sum(unnormed, -1, keepdims=True)))
        mixed_rows = jnp.einsum('kgqs,skd->qkgd', probability, value_rows, precision=PRECISE)
        return mixed_rows.reshape(block_rows, H * HD)
    attended = lax.map(jax.checkpoint(attend), (grouped, firsts)).reshape(length, H * HD)
    attended = low(low_back(attended))
    branch = low_back(jnp.dot(attended, out_weight, precision=PRECISE))
    middle = inputs + branch
    post_normed = low(norm_rows(middle, post_gain))
    gate_proj = low_back(jnp.dot(post_normed, gate_weight, precision=PRECISE))
    up_proj = low_back(jnp.dot(post_normed, up_weight, precision=PRECISE))
    hidden = low(jax.nn.silu(gate_proj) * up_proj)
    return middle + jnp.dot(hidden, down_weight, precision=PRECISE)

def all_layers(inputs, *weights):
    return jnp.stack([layer(inputs[index], *weights) for index in range(SEQS)], 0)

def to_sequence(array):
    width = array.shape[-1]
    return jnp.stack([jnp.concatenate([array[index, 0].reshape(-1, width), array[index, 1][::-1].reshape(-1, width)], 0) for index in range(SEQS)], 0)

def from_sequence(array):
    halves = array.shape[1] // 2
    width = array.shape[-1]
    front = array[:, :halves].reshape(SEQS, N_CTX, BLK, width)
    behind = array[:, halves:].reshape(SEQS, N_CTX, BLK, width)[:, ::-1]
    return jnp.stack([front, behind], 1)

def reference(tokens, norm_gain, query_weight, key_weight, value_weight, query_gain, key_gain, out_weight, post_gain, gate_weight, up_weight, down_weight, cotangent):
    inputs = to_sequence(tokens.astype(jnp.float32))
    output, pullback = jax.vjp(all_layers, inputs, norm_gain.astype(jnp.float32), query_weight.astype(jnp.float32), key_weight.astype(jnp.float32), value_weight.astype(jnp.float32), query_gain.astype(jnp.float32), key_gain.astype(jnp.float32), out_weight.astype(jnp.float32), post_gain.astype(jnp.float32), gate_weight.astype(jnp.float32), up_weight.astype(jnp.float32), down_weight.astype(jnp.float32))
    grads = pullback(to_sequence(cotangent.astype(jnp.float32)))
    return (from_sequence(output).astype(jnp.bfloat16), from_sequence(grads[0]).astype(jnp.bfloat16), grads[1], grads[2], grads[3], grads[4], grads[5], grads[6], grads[7], grads[8], grads[9], grads[10], grads[11])
```

```python
import jax
import jax.numpy as jnp
import numpy as np
from jax import lax
from jax.experimental import pallas as pl
from jax.experimental.pallas import tpu as pltpu
from jax.sharding import PartitionSpec as P

HD = 64
EPS = 1e-05
ROPE_BASE = 1000000.0
BF = jnp.bfloat16
F32 = jnp.float32
MESH = pl.DeviceIdType.MESH
FF = 1152
GX = 3 * FF
G2X = 768

NN = (((1,), (0,)), ((), ()))
NT = (((1,), (1,)), ((), ()))
TN = (((0,), (0,)), ((), ()))


def dot(a, b, dims=NN):
    return lax.dot_general(a, b, dims, preferred_element_type=F32)


def rope_constants():
    freq = ROPE_BASE ** (-np.arange(0, HD, 2) / HD)
    freq = np.tile(freq, 4)[None, :]
    rows = np.arange(64)[:, None] * freq
    blocks = np.arange(64)[:, None] * 64.0 * freq
    return [f(a).astype(np.float32) for a in (rows, blocks) for f in (np.cos, np.sin)]


def lanes(shape):
    return lax.broadcasted_iota(jnp.int32, shape, len(shape) - 1)


def swap_halves(u):
    return jnp.where(lanes(u.shape) % 64 < 32, pltpu.roll(u, 96, 1), pltpu.roll(u, 32, 1))


def head_mean(u):
    low = lanes(u.shape) < 64
    first = jnp.sum(jnp.where(low, u, 0.0), -1, keepdims=True)
    second = jnp.sum(jnp.where(low, 0.0, u), -1, keepdims=True)
    return jnp.where(low, first, second) * (1.0 / 64)


def head_norm(u, gain):
    return u * lax.rsqrt(head_mean(u * u) + EPS) * gain


def head_norm_back(u, gain, grads):
    inv = lax.rsqrt(head_mean(u * u) + EPS)
    scaled = grads * gain
    back = inv * (scaled - u * (inv * inv) * head_mean(scaled * u))
    return back, grads * u * inv


def row_inverse(u):
    return lax.rsqrt(jnp.mean(u * u, -1, keepdims=True) + EPS)


def row_norm_back(u, gain, grads):
    inv = row_inverse(u)
    scaled = grads * gain
    back = inv * (scaled - u * (inv * inv) * jnp.mean(scaled * u, -1, keepdims=True))
    return back, grads * u * inv


def to_diagonal(part, kv, ref):
    low = lanes((64, 128)) < 64
    for s in range(2):
        for h in range(2):
            a = part[(s * 2 + h) * 64 : (s * 2 + h + 1) * 64]
            b = pltpu.roll(a, 64, 1)
            first, second = (a, b) if kv == 0 else (b, a)
            keep = low if kv == 0 else jnp.logical_not(low)
            at = h * 256 + kv * 128
            ref[s, at : at + 64, :] = jnp.where(keep, first, 0.0).astype(ref.dtype)
            ref[s, at + 64 : at + 128, :] = jnp.where(keep, second, 0.0).astype(ref.dtype)


def from_diagonal(rows, kv):
    low = lanes((64, 128)) < 64
    a = rows[kv * 128 : kv * 128 + 64]
    b = rows[kv * 128 + 64 : kv * 128 + 128]
    if kv == 0:
        return jnp.where(low, a, pltpu.roll(b, 64, 1))
    return jnp.where(low, pltpu.roll(a, 64, 1), b)


def kernel(
    x, ng, wq, wk, wv, qg, kg, wo_in, pg, wg_in, wu_in, wd_in, gy, cr, sr, cb, sb,
    mixed_out, xgrad_out, gains_out, gate_out, up_out, down_out, attn_out,
    wg, wu, wd, wo_all, nrm, kv_all, kp, qp, ct, st_, qbd, dobd, ot, stats, att_all,
    mid, post, hid, gg, ug, pp, ppb, mpb, ipb, xr, ml, mgr, mixed_s, xg_s, dq, dql, kvl,
    g1, r1, ra1, rb1, dkv, r0, ra0, rb0, g2, r2, ra2, rb2, gv, gr,
    loc, kss, krs, xss, xrs, s1, q1, s0, q0, s2, q2, gss, grs,
):
    c = lax.axis_index("ctx")
    t = lax.axis_index("tp")
    cy = lax.div(c, 8)
    cz = lax.rem(lax.div(c, 2), 4)
    ck = lax.rem(c, 2)
    sib = 1 - ck

    def off(v, d):
        return lax.rem(v + d + 4, 4)

    def at_y(d):
        return ((off(cy, d) * 4 + cz) * 2 + ck, t)

    def at_z(d):
        return ((cy * 4 + off(cz, d)) * 2 + ck, t)

    def at_x(d):
        return (c, off(t, d))

    at_k = ((cy * 4 + cz) * 2 + sib, t)
    order = (1, 3, 2)

    barrier = pltpu.get_barrier_semaphore()
    for d in order:
        for peer in (at_x(d), at_y(d), at_z(d)):
            pl.semaphore_signal(barrier, inc=1, device_id=peer, device_id_type=MESH)
    pl.semaphore_signal(barrier, inc=1, device_id=at_k, device_id_type=MESH)

    locals_ = []
    for n, (src, dst) in enumerate(
        ((wo_in, wo_all.at[t]), (wg_in, wg), (wu_in, wu), (wd_in, wd))
    ):
        cp = pltpu.make_async_copy(src, dst, loc.at[n])
        cp.start()
        locals_.append(cp)

    sent = []

    def remote(src, dst, ssem, rsem, peer):
        cp = pltpu.make_async_remote_copy(
            src_ref=src, dst_ref=dst, send_sem=ssem, recv_sem=rsem, device_id=peer, device_id_type=MESH
        )
        cp.start()
        sent.append(cp)
        return cp

    xf = x[...].astype(F32)
    nrm[...] = (xf * row_inverse(xf) * ng[...]).astype(BF)
    lane64 = lanes((64, 128))
    sign = jnp.where(lane64 % 64 < 32, -1.0, 1.0)
    for h in range(2):
        place = c if h == 0 else 63 - c
        cos_b, sin_b = cb[pl.ds(place, 1), :], sb[pl.ds(place, 1), :]
        cos_h = cos_b * cr[...] - sin_b * sr[...]
        sin_h = (sin_b * cr[...] + cos_b * sr[...]) * sign
        for s in range(2):
            ct[pl.ds((s * 2 + h) * 64, 64), :] = cos_h
            st_[pl.ds((s * 2 + h) * 64, 64), :] = sin_h

    def rotate(u):
        return u * ct[...] + swap_halves(u) * st_[...]

    def rotate_back(u):
        return u * ct[...] - swap_halves(u) * st_[...]

    kproj = dot(nrm[...], wk[...])
    kp[...] = kproj
    kv_all[0, c] = rotate(head_norm(kproj, kg[...])).astype(BF)
    kv_all[1, c] = dot(nrm[...], wv[...]).astype(BF)

    pl.semaphore_wait(barrier, 10)

    arrive = {}

    def pass_on(kind, dy, dz, axis, d):
        source = (off(cy, -dy) * 4 + off(cz, -dz)) * 2 + ck
        if axis == "y":
            key, peer = (dy + d, dz, 0), at_y(d)
        elif axis == "z":
            key, peer = (dy, dz + d, 0), at_z(d)
        else:
            key, peer = (dy, dz, 1), at_k
        n = (key[0] * 4 + key[1]) * 2 + key[2]
        ref = kv_all.at[kind, source]
        arrive[kind, key] = remote(ref, ref, kss.at[kind, n], krs.at[kind, n], peer)

    for d in order:
        pass_on(0, 0, 0, "y", d)
        pass_on(1, 0, 0, "z", d)
    for kind in range(2):
        pass_on(kind, 0, 0, "k", 1)
    for d in order:
        pass_on(0, 0, 0, "z", d)
        pass_on(1, 0, 0, "y", d)

    locals_[0].wait()
    wo_c = [
        remote(wo_all.at[t], wo_all.at[t], xss.at[0, d - 1], xrs.at[0, d - 1], at_x(d)) for d in order
    ]

    for kv in range(2):
        proj = dot(nrm[...], wq[:, kv * 128 : (kv + 1) * 128])
        qp[kv] = proj
        to_diagonal(rotate(head_norm(proj, qg[...])).astype(BF).astype(F32) * 0.125, kv, qbd)

    for d in order:
        arrive[0, (d, 0, 0)].wait_recv()
        for e in order:
            pass_on(0, d, 0, "z", e)
        pass_on(0, d, 0, "k", 1)
        arrive[1, (0, d, 0)].wait_recv()
        for e in order:
            pass_on(1, 0, d, "y", e)
        pass_on(1, 0, d, "k", 1)
    for a in (0, 1, 3, 2):
        for b in order:
            arrive[0, (a, b, 0)].wait_recv()
            pass_on(0, a, b, "k", 1)
            arrive[1, (b, a, 0)].wait_recv()
            pass_on(1, b, a, "k", 1)
    for kind in range(2):
        for dy in range(4):
            for dz in range(4):
                arrive[kind, (dy, dz, 1)].wait_recv()

    own_chunk = cy

    def chunk(kind, j, s, kh):
        return kv_all[kind, pl.ds(j * 8, 8), pl.ds((s * 2 + kh) * 64, 64), :].reshape(512, 128)

    def visible_front(j, width):
        keys = j * 512 + lax.broadcasted_iota(jnp.int32, (512, width), 0)
        lane = lax.broadcasted_iota(jnp.int32, (512, width), 1)
        return (keys <= c * 64 + lane % 64) | (lane >= 256)

    def visible_back(j):
        keys = lax.broadcasted_iota(jnp.int32, (512, 256), 0)
        lane = lax.broadcasted_iota(jnp.int32, (512, 256), 1)
        return keys % 64 - 64 * (j * 8 + keys // 64) <= lane % 64 - 64 * c

    def forward_step(j, carry, h, kh, mask):
        out = []
        seen = mask(j) if mask is not None else None
        for s in range(2):
            m, l = carry[s]
            scores = dot(chunk(0, j, s, kh), qbd[s, h * 256 : (h + 1) * 256, :], NT)
            if seen is not None:
                scores = jnp.where(seen, scores, -1e30)
            new = jnp.maximum(m, jnp.max(scores, 0, keepdims=True))
            p = jnp.exp(scores - new)
            scale = jnp.exp(m - new)
            l = l * scale + jnp.sum(p, 0, keepdims=True)
            ot[s, :, h * 256 : (h + 1) * 256] = ot[s, :, h * 256 : (h + 1) * 256] * scale + dot(
                chunk(1, j, s, kh), p.astype(BF), TN
            )
            out.append((new, l))
        return tuple(out)

    ot[...] = jnp.zeros_like(ot)
    start = tuple((jnp.full((1, 256), -1e30, F32), jnp.zeros((1, 256), F32)) for _ in range(2))
    totals = [None, None]
    totals[0] = lax.fori_loop(
        0, own_chunk + 1, lambda j, v: forward_step(j, v, 0, 0, lambda n: visible_front(n, 256)), start
    )
    run = lax.fori_loop(0, 4, lambda j, v: forward_step(j, v, 1, 0, None), start)
    totals[1] = lax.fori_loop(
        own_chunk, 4, lambda j, v: forward_step(j, v, 1, 1, visible_back), run
    )
    for s in range(2):
        for h in range(2):
            m, l = totals[h][s]
            cols = slice(h * 256, (h + 1) * 256)
            o = ot[s, :, cols] / l
            ot[s, :, cols] = o
            stats[s, 0:1, cols] = m + jnp.log(l)
            rows = o.T
            for kv in range(2):
                att_all[t, pl.ds((s * 2 + h) * 64, 64), kv * 128 : (kv + 1) * 128] = from_diagonal(
                    rows, kv
                ).astype(BF)

    att_c = [
        remote(att_all.at[t], att_all.at[t], xss.at[1, d - 1], xrs.at[1, d - 1], at_x(d)) for d in order
    ]
    for cp in locals_[1:]:
        cp.wait()
    for cp in wo_c:
        cp.wait_recv()
    for cp in att_c:
        cp.wait_recv()

    branch = dot(att_all[0], wo_all[0])
    for n in range(1, 4):
        branch = branch + dot(att_all[n], wo_all[n])
    mid[...] = x[...].astype(F32) + branch
    post[...] = (mid[...] * row_inverse(mid[...]) * pg[...]).astype(BF)

    pp[...] = jnp.zeros_like(pp)

    def mlp_step(n, _):
        cols = pl.ds(pl.multiple_of(n * 384, 128), 384)
        g = dot(post[...], wg[:, cols])
        u = dot(post[...], wu[:, cols])
        hgrad = dot(gy[...], wd[cols, :], NT)
        sg = 1.0 / (1.0 + jnp.exp(-g))
        silu = g * sg
        hid[:, cols] = (silu * u).astype(BF)
        a = (hgrad * u * sg * (1.0 + g * (1.0 - sg))).astype(BF)
        b = (hgrad * silu).astype(BF)
        gg[:, cols] = a
        ug[:, cols] = b
        pp[...] += dot(a, wg[:, cols], NT) + dot(b, wu[:, cols], NT)
        return 0

    lax.fori_loop(0, 3, mlp_step, 0)

    def rows_of(n):
        return pl.ds(pl.multiple_of(n * 64, 64), 64)

    def scatter_x(src, n):
        return [
            remote(src.at[rows_of(off(t, d))], xr.at[n - 2, d - 1], xss.at[n, d - 1], xrs.at[n, d - 1], at_x(d))
            for d in order
        ]

    def collect_x(src, n, copies):
        total = src[rows_of(t), :].astype(F32)
        for cp in copies:
            cp.wait_recv()
        for d in range(3):
            total = total + xr[n - 2, d].astype(F32)
        return total

    def spread_x(buf, n):
        return [
            remote(buf.at[rows_of(t)], buf.at[rows_of(t)], xss.at[n, d - 1], xrs.at[n, d - 1], at_x(d))
            for d in order
        ]

    ppb[...] = pp[...].astype(BF)
    post_c = scatter_x(ppb, 2)
    mpb[...] = dot(hid[...], wd[...]).astype(BF)
    mlp_c = scatter_x(mpb, 3)

    def core_stage(g, r, ss, qs, y):
        return remote(g.at[y, :, sib], r.at[y], ss.at[y], qs.at[y], at_k)

    def core_sum(g, r, y, copy):
        copy.wait_recv()

        def add(z, _):
            r[y, z] = (g[y, z, ck].astype(F32) + r[y, z].astype(F32)).astype(BF)
            return 0

        lax.fori_loop(0, 4, add, 0)

    def first_stage(r, ra, ss, qs):
        out = []
        for d in order:
            out.append(remote(r.at[off(cy, d), :, 0], ra.at[0, d - 1], ss.at[3 + d], qs.at[3 + d], at_y(d)))
            out.append(remote(r.at[:, off(cz, d), 1], ra.at[1, d - 1], ss.at[6 + d], qs.at[6 + d], at_z(d)))
        return out

    def first_sum(r, ra, copies):
        for cp in copies:
            cp.wait_recv()

        def add(n, _):
            for half, at in ((0, (cy, n)), (1, (n, cz))):
                total = r[at[0], at[1], half].astype(F32)
                for d in range(3):
                    total = total + ra[half, d, n].astype(F32)
                r[at[0], at[1], half] = total.astype(BF)
            return 0

        lax.fori_loop(0, 4, add, 0)

    def second_stage(r, rb, ss, qs):
        out = []
        for d in order:
            out.append(remote(r.at[cy, off(cz, d), 0], rb.at[0, d - 1], ss.at[9 + d], qs.at[9 + d], at_z(d)))
            out.append(remote(r.at[off(cy, d), cz, 1], rb.at[1, d - 1], ss.at[12 + d], qs.at[12 + d], at_y(d)))
        return out

    def second_sum(r, rb, copies):
        for cp in copies:
            cp.wait_recv()
        out = []
        for half in range(2):
            total = r[cy, cz, half].astype(F32)
            for d in range(3):
                total = total + rb[half, d].astype(F32)
            out.append(total)
        return out

    core1 = []
    for y in range(4):
        cols = slice(y * 256, (y + 1) * 256)
        for n, (a, b) in enumerate(((post, gg), (post, ug), (gy, hid))):
            part = dot(a[:, cols], b[...], TN).astype(BF)
            g1[y, :, :, :, :, n * FF : (n + 1) * FF] = part.reshape(4, 2, 2, 16, FF)
        core1.append(core_stage(g1, r1, s1, q1, y))

    post_grad = collect_x(ppb, 2, post_c)
    back, post_gain_term = row_norm_back(mid[rows_of(t), :], pg[...], post_grad)
    mgr[...] = gy[rows_of(t), :].astype(F32) + back
    ml[rows_of(t), :] = mgr[...].astype(BF)
    ml_c = spread_x(ml, 4)
    gv[0, 1:2, :] = jnp.sum(post_gain_term, 0, keepdims=True)

    mixed_s[rows_of(t), :] = (mid[rows_of(t), :] + collect_x(mpb, 3, mlp_c)).astype(BF)
    mixed_c = spread_x(mixed_s, 5)

    for y in range(4):
        core_sum(g1, r1, y, core1[y])
    first1 = first_stage(r1, ra1, s1, q1)

    for cp in ml_c:
        cp.wait_recv()

    ag = dot(ml[...], wo_all[t], NT).astype(BF).astype(F32)
    for kv in range(2):
        to_diagonal(ag[:, kv * 128 : (kv + 1) * 128], kv, dobd)
    for s in range(2):
        stats[s, 1:2, :] = jnp.sum(dobd[s].astype(F32).T * ot[s], 0, keepdims=True)
    dq[...] = jnp.zeros_like(dq)

    def back_step(j, s, kh, first, mask):
        at = slice(first, 512)
        kc, vc = chunk(0, j, s, kh), chunk(1, j, s, kh)
        q, do = qbd[s, at, :], dobd[s, at, :]
        p = jnp.exp(dot(kc, q, NT) - stats[s, 0:1, at])
        if mask is not None:
            p = jnp.where(mask(j), p, 0.0)
        ds = (p * (dot(vc, do, NT) - stats[s, 1:2, at])).astype(BF)
        where = pl.ds((s * 2 + kh) * 64, 64)
        dkv[j, :, :, 1, where, :] = dot(p.astype(BF), do).astype(BF).reshape(4, 2, 64, 128)
        dkv[j, :, :, 0, where, :] = dot(ds, q).astype(BF).reshape(4, 2, 64, 128)
        dq[s, at, :] += dot(ds, kc, TN)

    def front_both(j, _):
        for s in range(2):
            back_step(j, s, 0, 0, lambda n: visible_front(n, 512))
        return 0

    def front_one(j, _):
        for s in range(2):
            back_step(j, s, 0, 256, None)
        return 0

    def behind_one(j, _):
        for s in range(2):
            back_step(j, s, 1, 256, visible_back)
        return 0

    def behind_none(j, _):
        for s in range(2):
            for kind in range(2):
                dkv[j, :, :, kind, pl.ds((s * 2 + 1) * 64, 64), :] = jnp.zeros((4, 2, 64, 128), BF)
        return 0

    lax.fori_loop(0, own_chunk, behind_none, 0)
    lax.fori_loop(0, own_chunk + 1, front_both, 0)
    lax.fori_loop(own_chunk + 1, 4, front_one, 0)
    lax.fori_loop(own_chunk, 4, behind_one, 0)

    core0 = [core_stage(dkv, r0, s0, q0, y) for y in range(4)]

    query_gain_term = jnp.zeros((1, 128), F32)
    for kv in range(2):
        parts = [
            from_diagonal(dq[s, h * 256 : (h + 1) * 256, :], kv) for s in range(2) for h in range(2)
        ]
        grads = rotate_back(jnp.concatenate(parts, 0) * 0.125)
        back, term = head_norm_back(qp[kv], qg[...], grads)
        dql[:, kv * 128 : (kv + 1) * 128] = back.astype(BF)
        query_gain_term = query_gain_term + jnp.sum(term, 0, keepdims=True)

    for y in range(4):
        core_sum(dkv, r0, y, core0[y])
    first0 = first_stage(r0, ra0, s0, q0)

    first_sum(r1, ra1, first1)
    second1 = second_stage(r1, rb1, s1, q1)

    def weight_part(lhs, rhs, at, y):
        width = rhs.shape[1]
        part = dot(lhs[:, y * 256 : (y + 1) * 256], rhs, TN).astype(BF)
        g2[y, :, :, :, :, at : at + width] = part.reshape(4, 2, 2, 16, width)

    own_att = att_all[t]
    for y in range(4):
        weight_part(ml, own_att, 512, y)
        weight_part(nrm, dql[...], 0, y)
    pp[...] = dot(dql[...], wq[...], NT)

    first_sum(r0, ra0, first0)
    second0 = second_stage(r0, rb0, s0, q0)

    for half, total in enumerate(second_sum(r1, rb1, second1)):
        rows = slice(half * 16, half * 16 + 16)
        for n, ref in enumerate((gate_out, up_out, down_out)):
            ref[rows, :] = total[:, n * FF : (n + 1) * FF]

    key_grad, value_grad = second_sum(r0, rb0, second0)
    back, term = head_norm_back(kp[...], kg[...], rotate_back(key_grad))
    kvl[:, 0:128] = back.astype(BF)
    kvl[:, 128:256] = value_grad.astype(BF)
    key_gain_term = jnp.sum(term, 0, keepdims=True)

    ipb[...] = (pp[...] + dot(kvl[:, 0:128], wk[...], NT) + dot(kvl[:, 128:256], wv[...], NT)).astype(BF)
    in_c = [
        remote(ipb.at[rows_of(off(t, d))], xr.at[2, d - 1], xss.at[6, d - 1], xrs.at[6, d - 1], at_x(d))
        for d in order
    ]
    core2 = []
    for y in range(4):
        weight_part(nrm, kvl[...], 256, y)
        core2.append(core_stage(g2, r2, s2, q2, y))
    total = ipb[rows_of(t), :].astype(F32)
    for cp in in_c:
        cp.wait_recv()
    for d in range(3):
        total = total + xr[2, d].astype(F32)
    back, term = row_norm_back(x[rows_of(t), :].astype(F32), ng[...], total)
    xg_s[rows_of(t), :] = (mgr[...] + back).astype(BF)
    xg_c = [
        remote(xg_s.at[rows_of(t)], xg_s.at[rows_of(t)], xss.at[7, d - 1], xrs.at[7, d - 1], at_x(d))
        for d in order
    ]
    gv[0, 0:1, :] = jnp.sum(term, 0, keepdims=True)
    gv[0, 2:8, :] = jnp.zeros((6, 1024), F32)
    gv[0, 2:3, 0:128] = query_gain_term + pltpu.roll(query_gain_term, 64, 1)
    gv[0, 3:4, 0:128] = key_gain_term + pltpu.roll(key_gain_term, 64, 1)

    def gain_stage(n, peers):
        base = (0, 1, 4, 7)[n]
        return [
            remote(gv.at[n], gr.at[base + i], gss.at[base + i], grs.at[base + i], peer)
            for i, peer in enumerate(peers)
        ]

    def gain_sum(n, copies):
        base = (0, 1, 4, 7)[n]
        total = gv[n]
        for i, cp in enumerate(copies):
            cp.wait_recv()
            total = total + gr[base + i]
        return total

    gain_c = gain_stage(0, [at_k])
    for y in range(4):
        core_sum(g2, r2, y, core2[y])
    first2 = first_stage(r2, ra2, s2, q2)
    gv[1] = gain_sum(0, gain_c)
    gain_c = gain_stage(1, [at_x(d) for d in order])
    first_sum(r2, ra2, first2)
    second2 = second_stage(r2, rb2, s2, q2)
    gv[2] = gain_sum(1, gain_c)
    gain_c = gain_stage(2, [at_y(d) for d in order])
    for half, total in enumerate(second_sum(r2, rb2, second2)):
        attn_out[half * 16 : half * 16 + 16, :] = total
    gv[3] = gain_sum(2, gain_c)
    gain_c = gain_stage(3, [at_z(d) for d in order])
    for cp in mixed_c:
        cp.wait_recv()
    mixed_out[...] = mixed_s[...]
    for cp in xg_c:
        cp.wait_recv()
    xgrad_out[...] = xg_s[...]
    gains_out[...] = gain_sum(3, gain_c)
    for cp in sent:
        cp.wait_send()


def on_device(
    tokens, norm_gain, query_weight, key_weight, value_weight, query_gain, key_gain, out_weight,
    post_gain, gate_weight, up_weight, down_weight, cotangent,
):
    x = tokens.reshape(256, 1024)
    gy = cotangent.reshape(256, 1024)
    tables = [jnp.asarray(a) for a in rope_constants()]
    cr, sr, cb, sb = tables
    vm = pl.BlockSpec(memory_space=pltpu.VMEM)
    hbm = pl.BlockSpec(memory_space=pl.ANY)
    V = pltpu.VMEM
    sem = lambda *s: pltpu.SemaphoreType.DMA(s)
    scratch = [
        V((1024, FF), BF), V((1024, FF), BF), V((FF, 1024), BF), V((4, 256, 1024), BF),
        V((256, 1024), BF), V((2, 32, 256, 128), BF), V((256, 128), F32), V((2, 256, 128), F32),
        V((256, 128), F32), V((256, 128), F32), V((2, 512, 128), BF), V((2, 512, 128), BF),
        V((2, 128, 512), F32), V((2, 8, 512), F32), V((4, 256, 256), BF),
        V((256, 1024), F32), V((256, 1024), BF), V((256, FF), BF), V((256, FF), BF), V((256, FF), BF),
        V((256, 1024), F32), V((256, 1024), BF), V((256, 1024), BF), V((256, 1024), BF),
        V((3, 3, 64, 1024), BF),
        V((256, 1024), BF), V((64, 1024), F32), V((256, 1024), BF), V((256, 1024), BF),
        V((2, 512, 128), F32), V((256, 256), BF), V((256, 256), BF),
        V((4, 4, 2, 2, 16, GX), BF), V((4, 4, 2, 16, GX), BF), V((2, 3, 4, 16, GX), BF), V((2, 3, 16, GX), BF),
        V((4, 4, 2, 2, 256, 128), BF), V((4, 4, 2, 256, 128), BF), V((2, 3, 4, 256, 128), BF), V((2, 3, 256, 128), BF),
        V((4, 4, 2, 2, 16, G2X), BF), V((4, 4, 2, 16, G2X), BF), V((2, 3, 4, 16, G2X), BF), V((2, 3, 16, G2X), BF),
        V((4, 8, 1024), F32), V((10, 8, 1024), F32),
        sem(4), sem(2, 32), sem(2, 32), sem(8, 3), sem(8, 3),
        sem(16), sem(16), sem(16), sem(16), sem(16), sem(16), sem(10), sem(10),
    ]
    shape = jax.ShapeDtypeStruct
    mixed, xgrad, gains, gate, up, down, attn = pl.pallas_call(
        kernel,
        name="block",
        out_shape=[
            shape((256, 1024), BF), shape((256, 1024), BF), shape((8, 1024), F32),
            shape((32, FF), F32), shape((32, FF), F32), shape((32, FF), F32), shape((32, G2X), F32),
        ],
        in_specs=[vm] * 7 + [hbm] + [vm] + [hbm] * 3 + [vm] * 5,
        out_specs=[vm] * 7,
        scratch_shapes=scratch,
        compiler_params=pltpu.CompilerParams(
            collective_id=0, has_side_effects=True, vmem_limit_bytes=63 * 2**20
        ),
    )(
        x, norm_gain.reshape(1, 1024), query_weight, key_weight, value_weight,
        jnp.tile(query_gain, 2).reshape(1, 128), jnp.tile(key_gain, 2).reshape(1, 128),
        out_weight, post_gain.reshape(1, 1024), gate_weight, up_weight, down_weight, gy, cr, sr, cb, sb,
    )
    place = (2, 2, 1, 64, 1024)
    return (
        mixed.reshape(place), xgrad.reshape(place), gains[0], attn[:, 0:256], attn[:, 256:384],
        attn[:, 384:512], gains[2, 0:64], gains[3, 0:64], attn[:, 512:768].T, gains[1], gate, up, down.T,
    )


def solution(mesh):
    tok = P(None, None, "ctx", None, None)
    col = P(None, "tp")
    row = P("tp", None)
    return jax.shard_map(
        on_device,
        mesh=mesh,
        in_specs=(tok, P(), col, col, col, P(), P(), row, P(), col, col, row, tok),
        out_specs=(
            tok, tok, P(), P("ctx", "tp"), P("ctx", "tp"), P("ctx", "tp"), P(), P(), P("tp", "ctx"), P(),
            P("ctx", "tp"), P("ctx", "tp"), P("tp", "ctx"),
        ),
        check_vma=False,
    )
```

```python
import jax
import jax.numpy as jnp
import numpy as np
from jax import lax
from jax.experimental import pallas as pl
from jax.experimental.pallas import tpu as pltpu
from jax.sharding import PartitionSpec as P

HD = 64
EPS = 1e-05
ROPE_BASE = 1000000.0
BF = jnp.bfloat16
F32 = jnp.float32
MESH = pl.DeviceIdType.MESH
FF = 1152
G1X = 2 * FF
G2X = 256
G3X = FF + 512

NN = (((1,), (0,)), ((), ()))
NT = (((1,), (1,)), ((), ()))
TN = (((0,), (0,)), ((), ()))


def dot(a, b, dims=NN):
    return lax.dot_general(a, b, dims, preferred_element_type=F32)


def rope_constants():
    freq = ROPE_BASE ** (-np.arange(0, HD, 2) / HD)
    freq = np.tile(freq, 4)[None, :]
    rows = np.arange(64)[:, None] * freq
    blocks = np.arange(64)[:, None] * 64.0 * freq
    return [f(a).astype(np.float32) for a in (rows, blocks) for f in (np.cos, np.sin)]


def lanes(shape):
    return lax.broadcasted_iota(jnp.int32, shape, len(shape) - 1)


def swap_halves(u):
    return jnp.where(lanes(u.shape) % 64 < 32, pltpu.roll(u, 96, 1), pltpu.roll(u, 32, 1))


def head_mean(u):
    low = lanes(u.shape) < 64
    first = jnp.sum(jnp.where(low, u, 0.0), -1, keepdims=True)
    second = jnp.sum(jnp.where(low, 0.0, u), -1, keepdims=True)
    return jnp.where(low, first, second) * (1.0 / 64)


def head_norm(u, gain):
    return u * lax.rsqrt(head_mean(u * u) + EPS) * gain


def head_norm_back(u, gain, grads):
    inv = lax.rsqrt(head_mean(u * u) + EPS)
    scaled = grads * gain
    back = inv * (scaled - u * (inv * inv) * head_mean(scaled * u))
    return back, grads * u * inv


def row_inverse(u):
    return lax.rsqrt(jnp.mean(u * u, -1, keepdims=True) + EPS)


def row_norm_back(u, gain, grads):
    inv = row_inverse(u)
    scaled = grads * gain
    back = inv * (scaled - u * (inv * inv) * jnp.mean(scaled * u, -1, keepdims=True))
    return back, grads * u * inv


def to_diagonal(part, kv, ref):
    low = lanes((64, 128)) < 64
    for s in range(2):
        for h in range(2):
            a = part[(s * 2 + h) * 64 : (s * 2 + h + 1) * 64]
            b = pltpu.roll(a, 64, 1)
            first, second = (a, b) if kv == 0 else (b, a)
            keep = low if kv == 0 else jnp.logical_not(low)
            at = h * 256 + kv * 128
            ref[s, at : at + 64, :] = jnp.where(keep, first, 0.0).astype(ref.dtype)
            ref[s, at + 64 : at + 128, :] = jnp.where(keep, second, 0.0).astype(ref.dtype)


def from_diagonal(rows, kv):
    low = lanes((64, 128)) < 64
    a = rows[kv * 128 : kv * 128 + 64]
    b = rows[kv * 128 + 64 : kv * 128 + 128]
    if kv == 0:
        return jnp.where(low, a, pltpu.roll(b, 64, 1))
    return jnp.where(low, pltpu.roll(a, 64, 1), b)


def kernel(
    x, ng, wq, wk, wv, qg, kg, wo_in, pg, wg_in, wu_in, wd_in, gy, cr, sr, cb, sb,
    mixed_out, xgrad_out, ng_out, wq_out, wk_out, wv_out, qg_out, kg_out, wo_out, pg_out, gate_out, up_out, down_out,
    wg, wu, wd, wo_all, nrm, kv_all, kp, qp, ct, st_, qbd, dobd, ot, stats, att_all,
    mid, post, hid, gg, ug, pp, ppb, mpb, ipb, xr, ml, mgr, mixed_s, xg_s, dq, dql, kvl,
    g1, r1, ra1, rb1, dkv, r0, ra0, rb0, g2, r2, ra2, rb2, g3, r3, ra3, rb3, gv, gr,
    loc, kss, krs, xss, xrs, wss, wrs, s1, q1, s0, q0, s2, q2, s3, q3, bs0, bq0, gss, grs,
):
    c = lax.axis_index("ctx")
    t = lax.axis_index("tp")
    cy = lax.div(c, 8)
    cz = lax.rem(lax.div(c, 2), 4)
    ck = lax.rem(c, 2)
    sib = 1 - ck

    def off(v, d):
        return lax.rem(v + d + 4, 4)

    def at_y(d):
        return ((off(cy, d) * 4 + cz) * 2 + ck, t)

    def at_z(d):
        return ((cy * 4 + off(cz, d)) * 2 + ck, t)

    def at_x(d):
        return (c, off(t, d))

    at_k = ((cy * 4 + cz) * 2 + sib, t)
    order = (1, 3, 2)

    barrier = pltpu.get_barrier_semaphore()
    for d in order:
        for peer in (at_x(d), at_y(d), at_z(d)):
            pl.semaphore_signal(barrier, inc=1, device_id=peer, device_id_type=MESH)
    pl.semaphore_signal(barrier, inc=1, device_id=at_k, device_id_type=MESH)

    locals_ = []
    for n, (src, dst) in enumerate(
        ((wo_in, wo_all.at[t]), (wg_in, wg), (wu_in, wu), (wd_in, wd))
    ):
        cp = pltpu.make_async_copy(src, dst, loc.at[n])
        cp.start()
        locals_.append(cp)

    sent = []

    def remote_copy(src, dst, ssem, rsem, peer):
        return pltpu.make_async_remote_copy(
            src_ref=src, dst_ref=dst, send_sem=ssem, recv_sem=rsem, device_id=peer, device_id_type=MESH
        )

    def remote(src, dst, ssem, rsem, peer):
        cp = remote_copy(src, dst, ssem, rsem, peer)
        cp.start()
        sent.append(cp)
        return cp

    xf = x[...].astype(F32)
    nrm[...] = (xf * row_inverse(xf) * ng[...]).astype(BF)
    lane64 = lanes((64, 128))
    sign = jnp.where(lane64 % 64 < 32, -1.0, 1.0)
    for h in range(2):
        place = c if h == 0 else 63 - c
        cos_b, sin_b = cb[pl.ds(place, 1), :], sb[pl.ds(place, 1), :]
        cos_h = cos_b * cr[...] - sin_b * sr[...]
        sin_h = (sin_b * cr[...] + cos_b * sr[...]) * sign
        for s in range(2):
            ct[pl.ds((s * 2 + h) * 64, 64), :] = cos_h
            st_[pl.ds((s * 2 + h) * 64, 64), :] = sin_h

    def rotate(u):
        return u * ct[...] + swap_halves(u) * st_[...]

    def rotate_back(u):
        return u * ct[...] - swap_halves(u) * st_[...]

    key_gain = jnp.concatenate([kg[...], kg[...]], 1)
    query_gain = jnp.concatenate([qg[...], qg[...]], 1)
    kproj = dot(nrm[...], wk[...])
    kp[...] = kproj
    kv_all[0, c] = rotate(head_norm(kproj, key_gain)).astype(BF)
    kv_all[1, c] = dot(nrm[...], wv[...]).astype(BF)

    pl.semaphore_wait(barrier, 10)

    arrive = {}

    def pass_on(kind, dy, dz, axis, d):
        source = (off(cy, -dy) * 4 + off(cz, -dz)) * 2 + ck
        if axis == "y":
            key, peer = (dy + d, dz, 0), at_y(d)
        elif axis == "z":
            key, peer = (dy, dz + d, 0), at_z(d)
        else:
            key, peer = (dy, dz, 1), at_k
        n = (key[0] * 4 + key[1]) * 2 + key[2]
        ref = kv_all.at[kind, source]
        arrive[kind, key] = remote(ref, ref, kss.at[kind, n], krs.at[kind, n], peer)

    for d in order:
        pass_on(0, 0, 0, "y", d)
        pass_on(1, 0, 0, "z", d)
    for kind in range(2):
        pass_on(kind, 0, 0, "k", 1)
    for d in order:
        pass_on(0, 0, 0, "z", d)
        pass_on(1, 0, 0, "y", d)

    locals_[0].wait()
    def out_half(n):
        return wo_all.at[n, pl.ds(pl.multiple_of(ck * 128, 128), 128)]

    wo_c = [remote(out_half(t), out_half(t), xss.at[0, d - 1], xrs.at[0, d - 1], at_x(d)) for d in order]

    for kv in range(2):
        proj = dot(nrm[...], wq[:, kv * 128 : (kv + 1) * 128])
        qp[kv] = proj
        to_diagonal(rotate(head_norm(proj, query_gain)).astype(BF).astype(F32) * 0.125, kv, qbd)

    for d in order:
        arrive[0, (d, 0, 0)].wait_recv()
        for e in order:
            pass_on(0, d, 0, "z", e)
        pass_on(0, d, 0, "k", 1)
        arrive[1, (0, d, 0)].wait_recv()
        for e in order:
            pass_on(1, 0, d, "y", e)
        pass_on(1, 0, d, "k", 1)
    for a in (0, 1, 3, 2):
        for b in order:
            arrive[0, (a, b, 0)].wait_recv()
            pass_on(0, a, b, "k", 1)
            arrive[1, (b, a, 0)].wait_recv()
            pass_on(1, b, a, "k", 1)
    wo_k = []
    for d, cp in zip(order, wo_c):
        cp.wait_recv()
        half = out_half(off(t, -d))
        wo_k.append(remote(half, half, wss.at[d - 1], wrs.at[d - 1], at_k))
    for kind in range(2):
        for dy in range(4):
            for dz in range(4):
                arrive[kind, (dy, dz, 1)].wait_recv()

    own_chunk = cy

    def chunk(kind, j, s, kh):
        return kv_all[kind, pl.ds(j * 8, 8), pl.ds((s * 2 + kh) * 64, 64), :].reshape(512, 128)

    def visible_front(j, width):
        keys = j * 512 + lax.broadcasted_iota(jnp.int32, (512, width), 0)
        lane = lax.broadcasted_iota(jnp.int32, (512, width), 1)
        return (keys <= c * 64 + lane % 64) | (lane >= 256)

    def visible_back(j):
        keys = lax.broadcasted_iota(jnp.int32, (512, 256), 0)
        lane = lax.broadcasted_iota(jnp.int32, (512, 256), 1)
        return keys % 64 - 64 * (j * 8 + keys // 64) <= lane % 64 - 64 * c

    def forward_step(j, carry, h, kh, mask):
        out = []
        seen = mask(j) if mask is not None else None
        for s in range(2):
            m, l = carry[s]
            scores = dot(chunk(0, j, s, kh), qbd[s, h * 256 : (h + 1) * 256, :], NT)
            if seen is not None:
                scores = jnp.where(seen, scores, -1e30)
            new = jnp.maximum(m, jnp.max(scores, 0, keepdims=True))
            p = jnp.exp(scores - new)
            scale = jnp.exp(m - new)
            l = l * scale + jnp.sum(p, 0, keepdims=True)
            ot[s, :, h * 256 : (h + 1) * 256] = ot[s, :, h * 256 : (h + 1) * 256] * scale + dot(
                chunk(1, j, s, kh), p.astype(BF), TN
            )
            out.append((new, l))
        return tuple(out)

    ot[...] = jnp.zeros_like(ot)
    start = tuple((jnp.full((1, 256), -1e30, F32), jnp.zeros((1, 256), F32)) for _ in range(2))
    totals = [None, None]
    totals[0] = lax.fori_loop(
        0, own_chunk + 1, lambda j, v: forward_step(j, v, 0, 0, lambda n: visible_front(n, 256)), start
    )
    run = lax.fori_loop(0, 4, lambda j, v: forward_step(j, v, 1, 0, None), start)
    totals[1] = lax.fori_loop(
        own_chunk, 4, lambda j, v: forward_step(j, v, 1, 1, visible_back), run
    )
    for s in range(2):
        for h in range(2):
            m, l = totals[h][s]
            cols = slice(h * 256, (h + 1) * 256)
            o = ot[s, :, cols] / l
            ot[s, :, cols] = o
            stats[s, 0:1, cols] = m + jnp.log(l)
            rows = o.T
            for kv in range(2):
                att_all[t, pl.ds((s * 2 + h) * 64, 64), kv * 128 : (kv + 1) * 128] = from_diagonal(
                    rows, kv
                ).astype(BF)

    att_c = [
        remote(att_all.at[t], att_all.at[t], xss.at[1, d - 1], xrs.at[1, d - 1], at_x(d)) for d in order
    ]
    for cp in locals_[1:]:
        cp.wait()
    for cp in wo_k:
        cp.wait_recv()
    for cp in att_c:
        cp.wait_recv()

    branch = dot(att_all[0], wo_all[0])
    for n in range(1, 4):
        branch = branch + dot(att_all[n], wo_all[n])
    mid[...] = x[...].astype(F32) + branch
    post[...] = (mid[...] * row_inverse(mid[...]) * pg[...]).astype(BF)

    pp[...] = jnp.zeros_like(pp)

    def mlp_step(n, _):
        cols = pl.ds(pl.multiple_of(n * 384, 128), 384)
        g = dot(post[...], wg[:, cols])
        u = dot(post[...], wu[:, cols])
        hgrad = dot(gy[...], wd[cols, :], NT)
        sg = 1.0 / (1.0 + jnp.exp(-g))
        silu = g * sg
        hid[:, cols] = (silu * u).astype(BF)
        a = (hgrad * u * sg * (1.0 + g * (1.0 - sg))).astype(BF)
        b = (hgrad * silu).astype(BF)
        gg[:, cols] = a
        ug[:, cols] = b
        pp[...] += dot(a, wg[:, cols], NT) + dot(b, wu[:, cols], NT)
        return 0

    lax.fori_loop(0, 3, mlp_step, 0)

    def rows_of(n):
        return pl.ds(pl.multiple_of(n * 64, 64), 64)

    def scatter_x(src, n):
        return [
            remote(src.at[rows_of(off(t, d))], xr.at[n - 2, d - 1], xss.at[n, d - 1], xrs.at[n, d - 1], at_x(d))
            for d in order
        ]

    def collect_x(src, n, copies):
        total = src[rows_of(t), :].astype(F32)
        for cp in copies:
            cp.wait_recv()
        for d in range(3):
            total = total + xr[n - 2, d].astype(F32)
        return total

    def spread_x(buf, n):
        return [
            remote(buf.at[rows_of(t)], buf.at[rows_of(t)], xss.at[n, d - 1], xrs.at[n, d - 1], at_x(d))
            for d in order
        ]

    ppb[...] = pp[...].astype(BF)
    post_c = scatter_x(ppb, 2)
    mpb[...] = dot(hid[...], wd[...]).astype(BF)

    def core_stage(g, r, ss, qs, y):
        return remote(g.at[y, :, sib], r.at[y], ss.at[y], qs.at[y], at_k)

    def core_sum(g, r, y, copy):
        copy.wait_recv()

        def add(z, _):
            r[y, z] = (g[y, z, ck].astype(F32) + r[y, z].astype(F32)).astype(BF)
            return 0

        lax.fori_loop(0, 4, add, 0)

    def first_stage(r, ra, ss, qs):
        out = []
        for d in order:
            out.append(remote(r.at[off(cy, d), :, 0], ra.at[0, d - 1], ss.at[3 + d], qs.at[3 + d], at_y(d)))
            out.append(remote(r.at[:, off(cz, d), 1], ra.at[1, d - 1], ss.at[6 + d], qs.at[6 + d], at_z(d)))
        return out

    def first_sum(r, ra, copies):
        for cp in copies:
            cp.wait_recv()

        def add(n, _):
            for half, at in ((0, (cy, n)), (1, (n, cz))):
                total = r[at[0], at[1], half].astype(F32)
                for d in range(3):
                    total = total + ra[half, d, n].astype(F32)
                r[at[0], at[1], half] = total.astype(BF)
            return 0

        lax.fori_loop(0, 4, add, 0)

    def second_stage(r, rb, ss, qs):
        out = []
        for d in order:
            out.append(remote(r.at[cy, off(cz, d), 0], rb.at[0, d - 1], ss.at[9 + d], qs.at[9 + d], at_z(d)))
            out.append(remote(r.at[off(cy, d), cz, 1], rb.at[1, d - 1], ss.at[12 + d], qs.at[12 + d], at_y(d)))
        return out

    def second_sum(r, rb, copies):
        for cp in copies:
            cp.wait_recv()
        out = []
        for half in range(2):
            total = r[cy, cz, half].astype(F32)
            for d in range(3):
                total = total + rb[half, d].astype(F32)
            out.append(total)
        return out

    def weight_part(g, lhs, rhs, at, y):
        width = rhs.shape[1]
        part = dot(lhs[:, y * 256 : (y + 1) * 256], rhs[...], TN).astype(BF)
        g[y, :, :, :, :, at : at + width] = part.reshape(4, 2, 2, 16, width)

    core1 = []
    for y in range(4):
        weight_part(g1, post, gg, 0, y)
        weight_part(g1, post, ug, FF, y)
        core1.append(core_stage(g1, r1, s1, q1, y))

    post_grad = collect_x(ppb, 2, post_c)
    back, post_gain_term = row_norm_back(mid[rows_of(t), :], pg[...], post_grad)
    mgr[...] = gy[rows_of(t), :].astype(F32) + back
    ml[rows_of(t), :] = mgr[...].astype(BF)
    ml_c = spread_x(ml, 4)
    gv[0, 1:2, :] = jnp.sum(post_gain_term, 0, keepdims=True)

    for y in range(4):
        core_sum(g1, r1, y, core1[y])
    first1 = first_stage(r1, ra1, s1, q1)

    for y in range(4):
        weight_part(g3, gy, hid, 0, y)
    for cp in ml_c:
        cp.wait_recv()
    mlp_c = scatter_x(mpb, 3)

    ag = dot(ml[...], wo_all[t], NT).astype(BF).astype(F32)
    for kv in range(2):
        to_diagonal(ag[:, kv * 128 : (kv + 1) * 128], kv, dobd)
    for s in range(2):
        stats[s, 1:2, :] = jnp.sum(dobd[s].astype(F32).T * ot[s], 0, keepdims=True)
    dq[...] = jnp.zeros_like(dq)

    def back_step(j, s, kh, first, mask):
        at = slice(first, 512)
        kc, vc = chunk(0, j, s, kh), chunk(1, j, s, kh)
        q, do = qbd[s, at, :], dobd[s, at, :]
        p = jnp.exp(dot(kc, q, NT) - stats[s, 0:1, at])
        if mask is not None:
            p = jnp.where(mask(j), p, 0.0)
        ds = (p * (dot(vc, do, NT) - stats[s, 1:2, at])).astype(BF)
        where = pl.ds((s * 2 + kh) * 64, 64)
        dkv[j, :, :, 1, where, :] = dot(p.astype(BF), do).astype(BF).reshape(4, 2, 64, 128)
        dkv[j, :, :, 0, where, :] = dot(ds, q).astype(BF).reshape(4, 2, 64, 128)
        dq[s, at, :] += dot(ds, kc, TN)

    def key_core(j):
        return remote_copy(dkv.at[j, :, sib], r0.at[j], s0.at[j], q0.at[j], at_k)

    def key_along_y(j):
        d = lax.rem(j - cy + 4, 4)
        peer = ((j * 4 + cz) * 2 + ck, t)
        return remote_copy(r0.at[j, :, 0], ra0.at[0, d - 1], s0.at[3 + d], q0.at[3 + d], peer)

    def key_along_z(j):
        return [
            remote_copy(r0.at[j, off(cz, d), 1], ra0.at[1, d - 1, j], bs0.at[d - 1, j], bq0.at[d - 1, j], at_z(d))
            for d in order
        ]

    def key_step(j, _):
        @pl.when(j < 4)
        def _():
            @pl.when(j <= cy)
            def _():
                for s in range(2):
                    back_step(j, s, 0, 0, lambda n: visible_front(n, 512))

            @pl.when(j > cy)
            def _():
                for s in range(2):
                    back_step(j, s, 0, 256, None)

            @pl.when(j >= cy)
            def _():
                for s in range(2):
                    back_step(j, s, 1, 256, visible_back)

            @pl.when(j < cy)
            def _():
                for s in range(2):
                    for kind in range(2):
                        dkv[j, :, :, kind, pl.ds((s * 2 + 1) * 64, 64), :] = jnp.zeros((4, 2, 64, 128), BF)

            key_core(j).start()

        @pl.when(j > 0)
        def _():
            core_sum(dkv, r0, j - 1, key_core(j - 1))

            @pl.when(j - 1 != cy)
            def _():
                key_along_y(j - 1).start()

            for cp in key_along_z(j - 1):
                cp.start()

        return 0

    lax.fori_loop(0, 5, key_step, 0)
    first0 = []
    for y in range(4):
        sent.append(key_core(y))
        first0 += key_along_z(y)
    for d in order:
        first0.append(
            remote_copy(r0.at[off(cy, d), :, 0], ra0.at[0, d - 1], s0.at[3 + d], q0.at[3 + d], at_y(d))
        )
    sent.extend(first0)

    query_gain_term = jnp.zeros((1, 128), F32)
    for kv in range(2):
        parts = [
            from_diagonal(dq[s, h * 256 : (h + 1) * 256, :], kv) for s in range(2) for h in range(2)
        ]
        grads = rotate_back(jnp.concatenate(parts, 0) * 0.125)
        back, term = head_norm_back(qp[kv], query_gain, grads)
        dql[:, kv * 128 : (kv + 1) * 128] = back.astype(BF)
        query_gain_term = query_gain_term + jnp.sum(term, 0, keepdims=True)

    mixed_s[rows_of(t), :] = (mid[rows_of(t), :] + collect_x(mpb, 3, mlp_c)).astype(BF)
    mixed_c = spread_x(mixed_s, 5)

    first_sum(r0, ra0, first0)
    second0 = second_stage(r0, rb0, s0, q0)
    first_sum(r1, ra1, first1)
    second1 = second_stage(r1, rb1, s1, q1)

    core3 = []
    for y in range(4):
        weight_part(g3, ml, att_all.at[t], FF, y)
        weight_part(g3, nrm, dql, FF + 256, y)
        core3.append(core_stage(g3, r3, s3, q3, y))
    pp[...] = dot(dql[...], wq[...], NT)

    key_grad, value_grad = second_sum(r0, rb0, second0)
    back, term = head_norm_back(kp[...], key_gain, rotate_back(key_grad))
    kvl[:, 0:128] = back.astype(BF)
    kvl[:, 128:256] = value_grad.astype(BF)
    key_gain_term = jnp.sum(term, 0, keepdims=True)

    ipb[...] = (pp[...] + dot(kvl[:, 0:128], wk[...], NT) + dot(kvl[:, 128:256], wv[...], NT)).astype(BF)
    in_c = [
        remote(ipb.at[rows_of(off(t, d))], xr.at[2, d - 1], xss.at[6, d - 1], xrs.at[6, d - 1], at_x(d))
        for d in order
    ]
    for y in range(4):
        core_sum(g3, r3, y, core3[y])
    first3 = first_stage(r3, ra3, s3, q3)
    for y in range(4):
        weight_part(g2, nrm, kvl, 0, y)
    core2 = [core_stage(g2, r2, s2, q2, y) for y in range(4)]

    for half, total in enumerate(second_sum(r1, rb1, second1)):
        rows = slice(half * 16, half * 16 + 16)
        gate_out[rows, :] = total[:, 0:FF]
        up_out[rows, :] = total[:, FF : 2 * FF]
    for y in range(4):
        core_sum(g2, r2, y, core2[y])
    first2 = first_stage(r2, ra2, s2, q2)

    total = ipb[rows_of(t), :].astype(F32)
    for cp in in_c:
        cp.wait_recv()
    for d in range(3):
        total = total + xr[2, d].astype(F32)
    back, term = row_norm_back(x[rows_of(t), :].astype(F32), ng[...], total)
    gv[0, 0:1, :] = jnp.sum(term, 0, keepdims=True)
    gv[0, 2:8, :] = jnp.zeros((6, 1024), F32)
    gv[0, 2:3, 0:128] = query_gain_term + pltpu.roll(query_gain_term, 64, 1)
    gv[0, 3:4, 0:128] = key_gain_term + pltpu.roll(key_gain_term, 64, 1)

    bases = (0, 3, 4, 7)

    def gain_stage(n, peers):
        return [
            remote(gv.at[n], gr.at[bases[n] + i], gss.at[bases[n] + i], grs.at[bases[n] + i], peer)
            for i, peer in enumerate(peers)
        ]

    def gain_sum(n, copies):
        total = gv[n]
        for i, cp in enumerate(copies):
            cp.wait_recv()
            total = total + gr[bases[n] + i]
        return total

    gain_c = gain_stage(0, [at_x(d) for d in order])
    xg_s[rows_of(t), :] = (mgr[...] + back).astype(BF)
    xg_c = [
        remote(xg_s.at[rows_of(t)], xg_s.at[rows_of(t)], xss.at[7, d - 1], xrs.at[7, d - 1], at_x(d))
        for d in order
    ]
    gv[1] = gain_sum(0, gain_c)
    gain_c = gain_stage(1, [at_k])
    first_sum(r3, ra3, first3)
    second3 = second_stage(r3, rb3, s3, q3)
    gv[2] = gain_sum(1, gain_c)
    gain_c = gain_stage(2, [at_y(d) for d in order])
    first_sum(r2, ra2, first2)
    second2 = second_stage(r2, rb2, s2, q2)
    for cp in mixed_c:
        cp.wait_recv()
    mixed_out[...] = mixed_s[...]
    gv[3] = gain_sum(2, gain_c)
    gain_c = gain_stage(3, [at_z(d) for d in order])
    for half, total in enumerate(second_sum(r3, rb3, second3)):
        rows = slice(half * 16, half * 16 + 16)
        down_out[rows, :] = total[:, 0:FF]
        wo_out[rows, :] = total[:, FF : FF + 256]
        wq_out[rows, :] = total[:, FF + 256 : FF + 512]
    for half, total in enumerate(second_sum(r2, rb2, second2)):
        rows = slice(half * 16, half * 16 + 16)
        wk_out[rows, :] = total[:, 0:128]
        wv_out[rows, :] = total[:, 128:256]
    for cp in xg_c:
        cp.wait_recv()
    xgrad_out[...] = xg_s[...]
    gains = gain_sum(3, gain_c)
    ng_out[...] = gains[0:1, :]
    pg_out[...] = gains[1:2, :]
    qg_out[...] = gains[2:3, 0:64]
    kg_out[...] = gains[3:4, 0:64]
    for cp in sent:
        cp.wait_send()


def hand_out(*refs):
    count = len(refs) // 2
    for source, target in zip(refs[:count], refs[count:]):
        target[...] = source[...]


def on_device(
    tokens, norm_gain, query_weight, key_weight, value_weight, query_gain, key_gain, out_weight,
    post_gain, gate_weight, up_weight, down_weight, cotangent,
):
    x = tokens.reshape(256, 1024)
    gy = cotangent.reshape(256, 1024)
    tables = [jnp.asarray(a) for a in rope_constants()]
    cr, sr, cb, sb = tables
    vm = pl.BlockSpec(memory_space=pltpu.VMEM)
    hbm = pl.BlockSpec(memory_space=pl.ANY)
    V = pltpu.VMEM
    sem = lambda *s: pltpu.SemaphoreType.DMA(s)

    def ring(rows, width):
        return [V(lead + (rows, width), BF) for lead in ((4, 4, 2, 2), (4, 4, 2), (2, 3, 4), (2, 3))]

    scratch = [
        V((1024, FF), BF), V((1024, FF), BF), V((FF, 1024), BF), V((4, 256, 1024), BF),
        V((256, 1024), BF), V((2, 32, 256, 128), BF), V((256, 128), F32), V((2, 256, 128), F32),
        V((256, 128), F32), V((256, 128), F32), V((2, 512, 128), BF), V((2, 512, 128), BF),
        V((2, 128, 512), F32), V((2, 8, 512), F32), V((4, 256, 256), BF),
        V((256, 1024), F32), V((256, 1024), BF), V((256, FF), BF), V((256, FF), BF), V((256, FF), BF),
        V((256, 1024), F32), V((256, 1024), BF), V((256, 1024), BF), V((256, 1024), BF),
        V((3, 3, 64, 1024), BF),
        V((256, 1024), BF), V((64, 1024), F32), V((256, 1024), BF), V((256, 1024), BF),
        V((2, 512, 128), F32), V((256, 256), BF), V((256, 256), BF),
        *ring(16, G1X),
        *ring(256, 128),
        *ring(16, G2X),
        *ring(16, G3X),
        V((4, 8, 1024), F32), V((10, 8, 1024), F32),
        sem(4), sem(2, 32), sem(2, 32), sem(8, 3), sem(8, 3), sem(3), sem(3),
        *[sem(16)] * 8, sem(3, 4), sem(3, 4), sem(10), sem(10),
    ]
    shape = jax.ShapeDtypeStruct
    outs = [
        shape((256, 1024), BF), shape((256, 1024), BF), shape((1, 1024), F32),
        shape((32, 256), F32), shape((32, 128), F32), shape((32, 128), F32),
        shape((1, 64), F32), shape((1, 64), F32), shape((32, 256), F32), shape((1, 1024), F32),
        shape((32, FF), F32), shape((32, FF), F32), shape((32, FF), F32),
    ]
    results = pl.pallas_call(
        kernel,
        name="block",
        out_shape=outs,
        in_specs=[vm] * 7 + [hbm] + [vm] + [hbm] * 3 + [vm] * 5,
        out_specs=[vm] * 13,
        scratch_shapes=scratch,
        compiler_params=pltpu.CompilerParams(
            collective_id=0, has_side_effects=True, vmem_limit_bytes=63 * 2**20
        ),
    )(
        x, norm_gain.reshape(1, 1024), query_weight, key_weight, value_weight,
        query_gain.reshape(1, 64), key_gain.reshape(1, 64),
        out_weight, post_gain.reshape(1, 1024), gate_weight, up_weight, down_weight, gy, cr, sr, cb, sb,
    )
    results = pl.pallas_call(
        hand_out,
        name="hand_out",
        out_shape=outs,
        in_specs=[vm] * 13,
        out_specs=[vm] * 13,
    )(*results)
    mixed, xgrad, ng, wq, wk, wv, qg, kg, wo, pg, gate, up, down = results
    place = (2, 2, 1, 64, 1024)
    return (
        mixed.reshape(place), xgrad.reshape(place), ng.reshape(1024), wq, wk, wv, qg.reshape(64), kg.reshape(64),
        wo.T, pg.reshape(1024), gate, up, down.T,
    )


def solution(mesh):
    tok = P(None, None, "ctx", None, None)
    col = P(None, "tp")
    row = P("tp", None)
    return jax.shard_map(
        on_device,
        mesh=mesh,
        in_specs=(tok, P(), col, col, col, P(), P(), row, P(), col, col, row, tok),
        out_specs=(
            tok, tok, P(), P("ctx", "tp"), P("ctx", "tp"), P("ctx", "tp"), P(), P(), P("tp", "ctx"), P(),
            P("ctx", "tp"), P("ctx", "tp"), P("tp", "ctx"),
        ),
        check_vma=False,
    )
```

```python
import jax
import jax.numpy as jnp
import numpy as np
from jax import lax
from jax.experimental import pallas as pl
from jax.experimental.pallas import tpu as pltpu
from jax.sharding import PartitionSpec as P

HD = 64
EPS = 1e-05
ROPE_BASE = 1000000.0
BF = jnp.bfloat16
F32 = jnp.float32
MESH = pl.DeviceIdType.MESH
FF = 1152
G1X = 2 * FF
G2X = 256
G3X = FF + 512

NN = (((1,), (0,)), ((), ()))
NT = (((1,), (1,)), ((), ()))
TN = (((0,), (0,)), ((), ()))


def dot(a, b, dims=NN):
    return lax.dot_general(a, b, dims, preferred_element_type=F32)


def rope_constants():
    freq = ROPE_BASE ** (-np.arange(0, HD, 2) / HD)
    freq = np.tile(freq, 4)[None, :]
    rows = np.arange(64)[:, None] * freq
    blocks = np.arange(64)[:, None] * 64.0 * freq
    return [f(a).astype(np.float32) for a in (rows, blocks) for f in (np.cos, np.sin)]


def lanes(shape):
    return lax.broadcasted_iota(jnp.int32, shape, len(shape) - 1)


def swap_halves(u):
    return jnp.where(lanes(u.shape) % 64 < 32, pltpu.roll(u, 96, 1), pltpu.roll(u, 32, 1))


def head_mean(u):
    low = lanes(u.shape) < 64
    first = jnp.sum(jnp.where(low, u, 0.0), -1, keepdims=True)
    second = jnp.sum(jnp.where(low, 0.0, u), -1, keepdims=True)
    return jnp.where(low, first, second) * (1.0 / 64)


def head_norm(u, gain):
    return u * lax.rsqrt(head_mean(u * u) + EPS) * gain


def head_norm_back(u, gain, grads):
    inv = lax.rsqrt(head_mean(u * u) + EPS)
    scaled = grads * gain
    back = inv * (scaled - u * (inv * inv) * head_mean(scaled * u))
    return back, grads * u * inv


def row_inverse(u):
    return lax.rsqrt(jnp.mean(u * u, -1, keepdims=True) + EPS)


def row_norm_back(u, gain, grads):
    inv = row_inverse(u)
    scaled = grads * gain
    back = inv * (scaled - u * (inv * inv) * jnp.mean(scaled * u, -1, keepdims=True))
    return back, grads * u * inv


def to_diagonal(part, kv, ref):
    low = lanes((64, 128)) < 64
    for s in range(2):
        for h in range(2):
            a = part[(s * 2 + h) * 64 : (s * 2 + h + 1) * 64]
            b = pltpu.roll(a, 64, 1)
            first, second = (a, b) if kv == 0 else (b, a)
            keep = low if kv == 0 else jnp.logical_not(low)
            at = h * 256 + kv * 128
            ref[s, at : at + 64, :] = jnp.where(keep, first, 0.0).astype(ref.dtype)
            ref[s, at + 64 : at + 128, :] = jnp.where(keep, second, 0.0).astype(ref.dtype)


def from_diagonal(rows, kv):
    low = lanes((64, 128)) < 64
    a = rows[kv * 128 : kv * 128 + 64]
    b = rows[kv * 128 + 64 : kv * 128 + 128]
    if kv == 0:
        return jnp.where(low, a, pltpu.roll(b, 64, 1))
    return jnp.where(low, pltpu.roll(a, 64, 1), b)


def kernel(
    x, ng, wq, wk, wv, qg, kg, wo_in, pg, wg_in, wu_in, wd_in, gy, cr, sr, cb, sb,
    mixed_out, xgrad_out, ng_out, wq_out, wk_out, wv_out, qg_out, kg_out, wo_out, pg_out, gate_out, up_out, down_out,
    wg, wu, wd, wo_all, nrm, kv_all, kp, qp, ct, st_, qbd, dobd, ot, sums, stats, att_all,
    mid, post, hid, gg, ug, pp, ppb, mpb, ipb, xr, ml, mgr, mixed_s, xg_s, dq, dql, kvl,
    g1, r1, ra1, rb1, dkv, r0, ra0, rb0, g2, r2, ra2, rb2, g3, r3, ra3, rb3, gv, gr,
    loc, kss, krs, xss, xrs, wss, wrs, s1, q1, s0, q0, s2, q2, s3, q3, bs0, bq0, gss, grs,
):
    c = lax.axis_index("ctx")
    t = lax.axis_index("tp")
    cy = lax.div(c, 8)
    cz = lax.rem(lax.div(c, 2), 4)
    ck = lax.rem(c, 2)
    sib = 1 - ck

    def off(v, d):
        return lax.rem(v + d + 4, 4)

    def at_y(d):
        return ((off(cy, d) * 4 + cz) * 2 + ck, t)

    def at_z(d):
        return ((cy * 4 + off(cz, d)) * 2 + ck, t)

    def at_x(d):
        return (c, off(t, d))

    at_k = ((cy * 4 + cz) * 2 + sib, t)
    order = (1, 3, 2)

    barrier = pltpu.get_barrier_semaphore()
    for d in order:
        for peer in (at_x(d), at_y(d), at_z(d)):
            pl.semaphore_signal(barrier, inc=1, device_id=peer, device_id_type=MESH)
    pl.semaphore_signal(barrier, inc=1, device_id=at_k, device_id_type=MESH)

    locals_ = []
    for n, (src, dst) in enumerate(
        ((wo_in, wo_all.at[t]), (wg_in, wg), (wu_in, wu), (wd_in, wd))
    ):
        cp = pltpu.make_async_copy(src, dst, loc.at[n])
        cp.start()
        locals_.append(cp)

    sent = []

    def remote_copy(src, dst, ssem, rsem, peer):
        return pltpu.make_async_remote_copy(
            src_ref=src, dst_ref=dst, send_sem=ssem, recv_sem=rsem, device_id=peer, device_id_type=MESH
        )

    def remote(src, dst, ssem, rsem, peer):
        cp = remote_copy(src, dst, ssem, rsem, peer)
        cp.start()
        sent.append(cp)
        return cp

    xf = x[...].astype(F32)
    nrm[...] = (xf * row_inverse(xf) * ng[...]).astype(BF)
    lane64 = lanes((64, 128))
    sign = jnp.where(lane64 % 64 < 32, -1.0, 1.0)
    for h in range(2):
        place = c if h == 0 else 63 - c
        cos_b, sin_b = cb[pl.ds(place, 1), :], sb[pl.ds(place, 1), :]
        cos_h = cos_b * cr[...] - sin_b * sr[...]
        sin_h = (sin_b * cr[...] + cos_b * sr[...]) * sign
        for s in range(2):
            ct[pl.ds((s * 2 + h) * 64, 64), :] = cos_h
            st_[pl.ds((s * 2 + h) * 64, 64), :] = sin_h

    def rotate(u):
        return u * ct[...] + swap_halves(u) * st_[...]

    def rotate_back(u):
        return u * ct[...] - swap_halves(u) * st_[...]

    key_gain = jnp.concatenate([kg[...], kg[...]], 1)
    query_gain = jnp.concatenate([qg[...], qg[...]], 1)
    kproj = dot(nrm[...], wk[...])
    kp[...] = kproj
    kv_all[0, c] = rotate(head_norm(kproj, key_gain)).astype(BF)
    kv_all[1, c] = dot(nrm[...], wv[...]).astype(BF)

    pl.semaphore_wait(barrier, 10)

    arrive = {}

    def pass_on(kind, dy, dz, axis, d):
        source = (off(cy, -dy) * 4 + off(cz, -dz)) * 2 + ck
        if axis == "y":
            key, peer = (dy + d, dz, 0), at_y(d)
        elif axis == "z":
            key, peer = (dy, dz + d, 0), at_z(d)
        else:
            key, peer = (dy, dz, 1), at_k
        n = (key[0] * 4 + key[1]) * 2 + key[2]
        ref = kv_all.at[kind, source]
        arrive[kind, key] = remote(ref, ref, kss.at[kind, n], krs.at[kind, n], peer)

    for d in order:
        pass_on(0, 0, 0, "y", d)
        pass_on(1, 0, 0, "z", d)
    for kind in range(2):
        pass_on(kind, 0, 0, "k", 1)
    for d in order:
        pass_on(0, 0, 0, "z", d)
        pass_on(1, 0, 0, "y", d)

    locals_[0].wait()
    def out_half(n):
        return wo_all.at[n, pl.ds(pl.multiple_of(ck * 128, 128), 128)]

    wo_c = [remote(out_half(t), out_half(t), xss.at[8, d - 1], xrs.at[8, d - 1], at_x(d)) for d in order]

    for kv in range(2):
        proj = dot(nrm[...], wq[:, kv * 128 : (kv + 1) * 128])
        qp[kv] = proj
        to_diagonal(rotate(head_norm(proj, query_gain)).astype(BF).astype(F32) * 0.125, kv, qbd)

    def seq_rows(s, kh):
        return pl.ds(pl.multiple_of((s * 2 + kh) * 64, 64), 64)

    def chunk(kind, j, s, kh):
        return kv_all[kind, pl.ds(j * 8, 8), seq_rows(s, kh), :].reshape(512, 128)

    def visible_front(width):
        keys = lax.broadcasted_iota(jnp.int32, (512, width), 0)
        lane = lax.broadcasted_iota(jnp.int32, (512, width), 1)
        return (keys <= lax.rem(c, 8) * 64 + lane % 64) | (lane >= 256)

    def visible_back():
        keys = lax.broadcasted_iota(jnp.int32, (512, 256), 0)
        lane = lax.broadcasted_iota(jnp.int32, (512, 256), 1)
        return keys % 64 - 64 * (keys // 64) <= lane % 64 - 64 * lax.rem(c, 8)

    def tile(s, j, kh, h, seen):
        p = jnp.exp(dot(chunk(0, j, s, kh), qbd[s, pl.ds(pl.multiple_of(h * 256, 256), 256), :], NT))
        if seen is not None:
            p = jnp.where(seen, p, 0.0)
        sums[s, h, 0:1, :] += jnp.sum(p, 0, keepdims=True)
        ot[s, h] += dot(chunk(1, j, s, kh), p.astype(BF), TN)

    def attend(s, dy):
        j = off(cy, -dy)
        if dy == 0:
            tile(s, j, 0, 0, visible_front(256))
            tile(s, j, 0, 1, None)
            tile(s, j, 1, 1, visible_back())
        else:
            later = jnp.where(j > cy, 1, 0)
            tile(s, j, 0, 1, None)
            tile(s, j, later, later, None)

    def await_sibling(dy):
        for kind in range(2):
            for dz in range(4):
                arrive[kind, (dy, dz, 1)].wait_recv()

    ot[...] = jnp.zeros_like(ot)
    sums[...] = jnp.zeros_like(sums)
    for d in order:
        arrive[0, (d, 0, 0)].wait_recv()
        for e in order:
            pass_on(0, d, 0, "z", e)
        pass_on(0, d, 0, "k", 1)
    for d in order:
        arrive[1, (0, d, 0)].wait_recv()
        pass_on(1, 0, d, "k", 1)
    for d in order:
        for e in order:
            pass_on(1, 0, e, "y", d)

    def pass_row(dy):
        for e in order:
            arrive[0, (dy, e, 0)].wait_recv()
            pass_on(0, dy, e, "k", 1)
        if dy > 0:
            for e in (0,) + order:
                arrive[1, (dy, e, 0)].wait_recv()
                pass_on(1, dy, e, "k", 1)

    pass_row(0)
    await_sibling(0)
    for s in range(2):
        attend(s, 0)
    pass_row(1)
    pass_row(3)
    await_sibling(1)
    for s in range(2):
        attend(s, 1)
    wo_k = []
    for d, cp in zip(order, wo_c):
        cp.wait_recv()
        half = out_half(off(t, -d))
        wo_k.append(remote(half, half, wss.at[d - 1], wrs.at[d - 1], at_k))
    pass_row(2)
    await_sibling(3)
    for s in range(2):
        attend(s, 3)
    await_sibling(2)
    att_c = []
    for s in range(2):
        attend(s, 2)
        for h in range(2):
            l = sums[s, h, 0:1, :]
            o = ot[s, h] / l
            ot[s, h] = o
            stats[s, 0:1, h * 256 : (h + 1) * 256] = jnp.log(l)
            rows = o.T
            for kv in range(2):
                att_all[t, pl.ds((s * 2 + h) * 64, 64), kv * 128 : (kv + 1) * 128] = from_diagonal(
                    rows, kv
                ).astype(BF)
        part = att_all.at[t, pl.ds(s * 128, 128)]
        att_c += [remote(part, part, xss.at[s, d - 1], xrs.at[s, d - 1], at_x(d)) for d in order]

    for cp in locals_[1:]:
        cp.wait()
    for cp in wo_k:
        cp.wait_recv()
    for cp in att_c:
        cp.wait_recv()

    branch = dot(att_all[0], wo_all[0])
    for n in range(1, 4):
        branch = branch + dot(att_all[n], wo_all[n])
    mid[...] = x[...].astype(F32) + branch
    post[...] = (mid[...] * row_inverse(mid[...]) * pg[...]).astype(BF)

    pp[...] = jnp.zeros_like(pp)

    def mlp_step(n, _):
        cols = pl.ds(pl.multiple_of(n * 384, 128), 384)
        g = dot(post[...], wg[:, cols])
        u = dot(post[...], wu[:, cols])
        hgrad = dot(gy[...], wd[cols, :], NT)
        sg = 1.0 / (1.0 + jnp.exp(-g))
        silu = g * sg
        hid[:, cols] = (silu * u).astype(BF)
        a = (hgrad * u * sg * (1.0 + g * (1.0 - sg))).astype(BF)
        b = (hgrad * silu).astype(BF)
        gg[:, cols] = a
        ug[:, cols] = b
        pp[...] += dot(a, wg[:, cols], NT) + dot(b, wu[:, cols], NT)
        return 0

    lax.fori_loop(0, 3, mlp_step, 0)

    def rows_of(n):
        return pl.ds(pl.multiple_of(n * 64, 64), 64)

    def scatter_x(src, n):
        return [
            remote(src.at[rows_of(off(t, d))], xr.at[n - 2, d - 1], xss.at[n, d - 1], xrs.at[n, d - 1], at_x(d))
            for d in order
        ]

    def collect_x(src, n, copies):
        total = src[rows_of(t), :].astype(F32)
        for cp in copies:
            cp.wait_recv()
        for d in range(3):
            total = total + xr[n - 2, d].astype(F32)
        return total

    def spread_x(buf, n):
        return [
            remote(buf.at[rows_of(t)], buf.at[rows_of(t)], xss.at[n, d - 1], xrs.at[n, d - 1], at_x(d))
            for d in order
        ]

    ppb[...] = pp[...].astype(BF)
    post_c = scatter_x(ppb, 2)
    mpb[...] = dot(hid[...], wd[...]).astype(BF)

    def core_stage(g, r, ss, qs, y):
        return remote(g.at[y, :, sib], r.at[y], ss.at[y], qs.at[y], at_k)

    def core_sum(g, r, y, copy):
        copy.wait_recv()

        def add(z, _):
            r[y, z] = (g[y, z, ck].astype(F32) + r[y, z].astype(F32)).astype(BF)
            return 0

        lax.fori_loop(0, 4, add, 0)

    def first_stage(r, ra, ss, qs):
        out = []
        for d in order:
            out.append(remote(r.at[off(cy, d), :, 0], ra.at[0, d - 1], ss.at[3 + d], qs.at[3 + d], at_y(d)))
            out.append(remote(r.at[:, off(cz, d), 1], ra.at[1, d - 1], ss.at[6 + d], qs.at[6 + d], at_z(d)))
        return out

    def first_sum(r, ra, copies):
        for cp in copies:
            cp.wait_recv()

        def add(n, _):
            for half, at in ((0, (cy, n)), (1, (n, cz))):
                total = r[at[0], at[1], half].astype(F32)
                for d in range(3):
                    total = total + ra[half, d, n].astype(F32)
                r[at[0], at[1], half] = total.astype(BF)
            return 0

        lax.fori_loop(0, 4, add, 0)

    def second_stage(r, rb, ss, qs):
        out = []
        for d in order:
            out.append(remote(r.at[cy, off(cz, d), 0], rb.at[0, d - 1], ss.at[9 + d], qs.at[9 + d], at_z(d)))
            out.append(remote(r.at[off(cy, d), cz, 1], rb.at[1, d - 1], ss.at[12 + d], qs.at[12 + d], at_y(d)))
        return out

    def second_sum(r, rb, copies):
        for cp in copies:
            cp.wait_recv()
        out = []
        for half in range(2):
            total = r[cy, cz, half].astype(F32)
            for d in range(3):
                total = total + rb[half, d].astype(F32)
            out.append(total)
        return out

    def weight_part(g, lhs, rhs, at, y):
        width = rhs.shape[1]
        part = dot(lhs[:, y * 256 : (y + 1) * 256], rhs[...], TN).astype(BF)
        g[y, :, :, :, :, at : at + width] = part.reshape(4, 2, 2, 16, width)

    core1 = []
    for y in range(4):
        weight_part(g1, post, gg, 0, y)
        weight_part(g1, post, ug, FF, y)
        core1.append(core_stage(g1, r1, s1, q1, y))

    post_grad = collect_x(ppb, 2, post_c)
    back, post_gain_term = row_norm_back(mid[rows_of(t), :], pg[...], post_grad)
    mgr[...] = gy[rows_of(t), :].astype(F32) + back
    ml[rows_of(t), :] = mgr[...].astype(BF)
    ml_c = spread_x(ml, 4)
    gv[0, 1:2, :] = jnp.sum(post_gain_term, 0, keepdims=True)

    for y in range(4):
        core_sum(g1, r1, y, core1[y])
    first1 = first_stage(r1, ra1, s1, q1)

    for y in range(4):
        weight_part(g3, gy, hid, 0, y)
    for cp in ml_c:
        cp.wait_recv()
    mlp_c = scatter_x(mpb, 3)

    ag = dot(ml[...], wo_all[t], NT).astype(BF).astype(F32)
    for kv in range(2):
        to_diagonal(ag[:, kv * 128 : (kv + 1) * 128], kv, dobd)
    for s in range(2):
        for h in range(2):
            at = slice(h * 256, (h + 1) * 256)
            stats[s, 1:2, at] = jnp.sum(dobd[s, at, :].astype(F32).T * ot[s, h], 0, keepdims=True)
    dq[...] = jnp.zeros_like(dq)

    def back_step(j, s, kh, first, seen):
        at = slice(first, 512)
        kc, vc = chunk(0, j, s, kh), chunk(1, j, s, kh)
        q, do = qbd[s, at, :], dobd[s, at, :]
        p = jnp.exp(dot(kc, q, NT) - stats[s, 0:1, at])
        if seen is not None:
            p = jnp.where(seen, p, 0.0)
        ds = (p * (dot(vc, do, NT) - stats[s, 1:2, at])).astype(BF)
        where = pl.ds((s * 2 + kh) * 64, 64)
        dkv[j, :, :, 1, where, :] = dot(p.astype(BF), do).astype(BF).reshape(4, 2, 64, 128)
        dkv[j, :, :, 0, where, :] = dot(ds, q).astype(BF).reshape(4, 2, 64, 128)
        dq[s, at, :] += dot(ds, kc, TN)

    def key_core(j):
        return remote_copy(dkv.at[j, :, sib], r0.at[j], s0.at[j], q0.at[j], at_k)

    def key_along_y(j):
        d = lax.rem(j - cy + 4, 4)
        peer = ((j * 4 + cz) * 2 + ck, t)
        return remote_copy(r0.at[j, :, 0], ra0.at[0, d - 1], s0.at[3 + d], q0.at[3 + d], peer)

    def key_along_z(j):
        return [
            remote_copy(r0.at[j, off(cz, d), 1], ra0.at[1, d - 1, j], bs0.at[d - 1, j], bq0.at[d - 1, j], at_z(d))
            for d in order
        ]

    def key_step(n, _):
        j = off(cy, n + 1)

        @pl.when(n < 4)
        def _():
            @pl.when(j < cy)
            def _():
                for s in range(2):
                    back_step(j, s, 0, 0, None)
                    for kind in range(2):
                        dkv[j, :, :, kind, pl.ds((s * 2 + 1) * 64, 64), :] = jnp.zeros((4, 2, 64, 128), BF)

            @pl.when(j > cy)
            def _():
                for s in range(2):
                    back_step(j, s, 0, 256, None)
                    back_step(j, s, 1, 256, None)

            @pl.when(j == cy)
            def _():
                for s in range(2):
                    back_step(j, s, 0, 0, visible_front(512))
                    back_step(j, s, 1, 256, visible_back())

            key_core(j).start()

        @pl.when(n > 0)
        def _():
            done = off(cy, n)
            core_sum(dkv, r0, done, key_core(done))

            @pl.when(n < 4)
            def _():
                key_along_y(done).start()

            for cp in key_along_z(done):
                cp.start()

        return 0

    lax.fori_loop(0, 5, key_step, 0)
    first0 = []
    for y in range(4):
        sent.append(key_core(y))
        first0 += key_along_z(y)
    for d in order:
        first0.append(
            remote_copy(r0.at[off(cy, d), :, 0], ra0.at[0, d - 1], s0.at[3 + d], q0.at[3 + d], at_y(d))
        )
    sent.extend(first0)

    query_gain_term = jnp.zeros((1, 128), F32)
    for kv in range(2):
        parts = [
            from_diagonal(dq[s, h * 256 : (h + 1) * 256, :], kv) for s in range(2) for h in range(2)
        ]
        grads = rotate_back(jnp.concatenate(parts, 0) * 0.125)
        back, term = head_norm_back(qp[kv], query_gain, grads)
        dql[:, kv * 128 : (kv + 1) * 128] = back.astype(BF)
        query_gain_term = query_gain_term + jnp.sum(term, 0, keepdims=True)

    mixed_s[rows_of(t), :] = (mid[rows_of(t), :] + collect_x(mpb, 3, mlp_c)).astype(BF)
    mixed_c = spread_x(mixed_s, 5)

    first_sum(r0, ra0, first0)
    second0 = second_stage(r0, rb0, s0, q0)
    first_sum(r1, ra1, first1)
    second1 = second_stage(r1, rb1, s1, q1)

    core3 = []
    for y in range(4):
        weight_part(g3, ml, att_all.at[t], FF, y)
        weight_part(g3, nrm, dql, FF + 256, y)
        core3.append(core_stage(g3, r3, s3, q3, y))
    pp[...] = dot(dql[...], wq[...], NT)

    key_grad, value_grad = second_sum(r0, rb0, second0)
    back, term = head_norm_back(kp[...], key_gain, rotate_back(key_grad))
    kvl[:, 0:128] = back.astype(BF)
    kvl[:, 128:256] = value_grad.astype(BF)
    key_gain_term = jnp.sum(term, 0, keepdims=True)

    ipb[...] = (pp[...] + dot(kvl[:, 0:128], wk[...], NT) + dot(kvl[:, 128:256], wv[...], NT)).astype(BF)
    in_c = [
        remote(ipb.at[rows_of(off(t, d))], xr.at[2, d - 1], xss.at[6, d - 1], xrs.at[6, d - 1], at_x(d))
        for d in order
    ]
    for y in range(4):
        core_sum(g3, r3, y, core3[y])
    first3 = first_stage(r3, ra3, s3, q3)
    for y in range(4):
        weight_part(g2, nrm, kvl, 0, y)
    core2 = [core_stage(g2, r2, s2, q2, y) for y in range(4)]

    for half, total in enumerate(second_sum(r1, rb1, second1)):
        rows = slice(half * 16, half * 16 + 16)
        gate_out[rows, :] = total[:, 0:FF]
        up_out[rows, :] = total[:, FF : 2 * FF]
    for y in range(4):
        core_sum(g2, r2, y, core2[y])
    first2 = first_stage(r2, ra2, s2, q2)

    total = ipb[rows_of(t), :].astype(F32)
    for cp in in_c:
        cp.wait_recv()
    for d in range(3):
        total = total + xr[2, d].astype(F32)
    back, term = row_norm_back(x[rows_of(t), :].astype(F32), ng[...], total)
    gv[0, 0:1, :] = jnp.sum(term, 0, keepdims=True)
    gv[0, 2:8, :] = jnp.zeros((6, 1024), F32)
    gv[0, 2:3, 0:128] = query_gain_term + pltpu.roll(query_gain_term, 64, 1)
    gv[0, 3:4, 0:128] = key_gain_term + pltpu.roll(key_gain_term, 64, 1)

    bases = (0, 3, 4, 7)

    def gain_stage(n, peers):
        return [
            remote(gv.at[n], gr.at[bases[n] + i], gss.at[bases[n] + i], grs.at[bases[n] + i], peer)
            for i, peer in enumerate(peers)
        ]

    def gain_sum(n, copies):
        total = gv[n]
        for i, cp in enumerate(copies):
            cp.wait_recv()
            total = total + gr[bases[n] + i]
        return total

    gain_c = gain_stage(0, [at_x(d) for d in order])
    xg_s[rows_of(t), :] = (mgr[...] + back).astype(BF)
    xg_c = [
        remote(xg_s.at[rows_of(t)], xg_s.at[rows_of(t)], xss.at[7, d - 1], xrs.at[7, d - 1], at_x(d))
        for d in order
    ]
    gv[1] = gain_sum(0, gain_c)
    gain_c = gain_stage(1, [at_k])
    first_sum(r3, ra3, first3)
    second3 = second_stage(r3, rb3, s3, q3)
    gv[2] = gain_sum(1, gain_c)
    gain_c = gain_stage(2, [at_y(d) for d in order])
    first_sum(r2, ra2, first2)
    second2 = second_stage(r2, rb2, s2, q2)
    for cp in mixed_c:
        cp.wait_recv()
    mixed_out[...] = mixed_s[...]
    gv[3] = gain_sum(2, gain_c)
    gain_c = gain_stage(3, [at_z(d) for d in order])
    for half, total in enumerate(second_sum(r3, rb3, second3)):
        rows = slice(half * 16, half * 16 + 16)
        down_out[rows, :] = total[:, 0:FF]
        wo_out[rows, :] = total[:, FF : FF + 256]
        wq_out[rows, :] = total[:, FF + 256 : FF + 512]
    for half, total in enumerate(second_sum(r2, rb2, second2)):
        rows = slice(half * 16, half * 16 + 16)
        wk_out[rows, :] = total[:, 0:128]
        wv_out[rows, :] = total[:, 128:256]
    for cp in xg_c:
        cp.wait_recv()
    xgrad_out[...] = xg_s[...]
    gains = gain_sum(3, gain_c)
    ng_out[...] = gains[0:1, :]
    pg_out[...] = gains[1:2, :]
    qg_out[...] = gains[2:3, 0:64]
    kg_out[...] = gains[3:4, 0:64]
    for cp in sent:
        cp.wait_send()


def hand_out(*refs):
    count = len(refs) // 2
    for source, target in zip(refs[:count], refs[count:]):
        target[...] = source[...]


def on_device(
    tokens, norm_gain, query_weight, key_weight, value_weight, query_gain, key_gain, out_weight,
    post_gain, gate_weight, up_weight, down_weight, cotangent,
):
    x = tokens.reshape(256, 1024)
    gy = cotangent.reshape(256, 1024)
    tables = [jnp.asarray(a) for a in rope_constants()]
    cr, sr, cb, sb = tables
    vm = pl.BlockSpec(memory_space=pltpu.VMEM)
    hbm = pl.BlockSpec(memory_space=pl.ANY)
    V = pltpu.VMEM
    sem = lambda *s: pltpu.SemaphoreType.DMA(s)

    def ring(rows, width):
        return [V(lead + (rows, width), BF) for lead in ((4, 4, 2, 2), (4, 4, 2), (2, 3, 4), (2, 3))]

    scratch = [
        V((1024, FF), BF), V((1024, FF), BF), V((FF, 1024), BF), V((4, 256, 1024), BF),
        V((256, 1024), BF), V((2, 32, 256, 128), BF), V((256, 128), F32), V((2, 256, 128), F32),
        V((256, 128), F32), V((256, 128), F32), V((2, 512, 128), BF), V((2, 512, 128), BF),
        V((2, 2, 128, 256), F32), V((2, 2, 8, 256), F32), V((2, 8, 512), F32), V((4, 256, 256), BF),
        V((256, 1024), F32), V((256, 1024), BF), V((256, FF), BF), V((256, FF), BF), V((256, FF), BF),
        V((256, 1024), F32), V((256, 1024), BF), V((256, 1024), BF), V((256, 1024), BF),
        V((3, 3, 64, 1024), BF),
        V((256, 1024), BF), V((64, 1024), F32), V((256, 1024), BF), V((256, 1024), BF),
        V((2, 512, 128), F32), V((256, 256), BF), V((256, 256), BF),
        *ring(16, G1X),
        *ring(256, 128),
        *ring(16, G2X),
        *ring(16, G3X),
        V((4, 8, 1024), F32), V((10, 8, 1024), F32),
        sem(4), sem(2, 32), sem(2, 32), sem(9, 3), sem(9, 3), sem(3), sem(3),
        *[sem(16)] * 8, sem(3, 4), sem(3, 4), sem(10), sem(10),
    ]
    shape = jax.ShapeDtypeStruct
    outs = [
        shape((256, 1024), BF), shape((256, 1024), BF), shape((1, 1024), F32),
        shape((32, 256), F32), shape((32, 128), F32), shape((32, 128), F32),
        shape((1, 64), F32), shape((1, 64), F32), shape((32, 256), F32), shape((1, 1024), F32),
        shape((32, FF), F32), shape((32, FF), F32), shape((32, FF), F32),
    ]
    results = pl.pallas_call(
        kernel,
        name="block",
        out_shape=outs,
        in_specs=[vm] * 7 + [hbm] + [vm] + [hbm] * 3 + [vm] * 5,
        out_specs=[vm] * 13,
        scratch_shapes=scratch,
        compiler_params=pltpu.CompilerParams(
            collective_id=0, has_side_effects=True, vmem_limit_bytes=63 * 2**20
        ),
    )(
        x, norm_gain.reshape(1, 1024), query_weight, key_weight, value_weight,
        query_gain.reshape(1, 64), key_gain.reshape(1, 64),
        out_weight, post_gain.reshape(1, 1024), gate_weight, up_weight, down_weight, gy, cr, sr, cb, sb,
    )
    results = pl.pallas_call(
        hand_out,
        name="hand_out",
        out_shape=outs,
        in_specs=[vm] * 13,
        out_specs=[vm] * 13,
    )(*results)
    mixed, xgrad, ng, wq, wk, wv, qg, kg, wo, pg, gate, up, down = results
    place = (2, 2, 1, 64, 1024)
    return (
        mixed.reshape(place), xgrad.reshape(place), ng.reshape(1024), wq, wk, wv, qg.reshape(64), kg.reshape(64),
        wo.T, pg.reshape(1024), gate, up, down.T,
    )


def solution(mesh):
    tok = P(None, None, "ctx", None, None)
    col = P(None, "tp")
    row = P("tp", None)
    return jax.shard_map(
        on_device,
        mesh=mesh,
        in_specs=(tok, P(), col, col, col, P(), P(), row, P(), col, col, row, tok),
        out_specs=(
            tok, tok, P(), P("ctx", "tp"), P("ctx", "tp"), P("ctx", "tp"), P(), P(), P("tp", "ctx"), P(),
            P("ctx", "tp"), P("ctx", "tp"), P("tp", "ctx"),
        ),
        check_vma=False,
    )
```

```python
import jax
import jax.numpy as jnp
import numpy as np
from jax import lax
from jax.experimental import pallas as pl
from jax.experimental.pallas import tpu as pltpu
from jax.sharding import PartitionSpec as P

HD = 64
EPS = 1e-05
ROPE_BASE = 1000000.0
BF = jnp.bfloat16
F32 = jnp.float32
MESH = pl.DeviceIdType.MESH
FF = 1152
G1X = 2 * FF
G2X = 256
G3X = FF + 512

NN = (((1,), (0,)), ((), ()))
NT = (((1,), (1,)), ((), ()))
TN = (((0,), (0,)), ((), ()))


def dot(a, b, dims=NN):
    return lax.dot_general(a, b, dims, preferred_element_type=F32)


def rope_constants():
    freq = ROPE_BASE ** (-np.arange(0, HD, 2) / HD)
    freq = np.tile(freq, 4)[None, :]
    rows = np.arange(64)[:, None] * freq
    blocks = np.arange(64)[:, None] * 64.0 * freq
    return [f(a).astype(np.float32) for a in (rows, blocks) for f in (np.cos, np.sin)]


def lanes(shape):
    return lax.broadcasted_iota(jnp.int32, shape, len(shape) - 1)


def swap_halves(u):
    return jnp.where(lanes(u.shape) % 64 < 32, pltpu.roll(u, 96, 1), pltpu.roll(u, 32, 1))


def head_mean(u):
    low = lanes(u.shape) < 64
    first = jnp.sum(jnp.where(low, u, 0.0), -1, keepdims=True)
    second = jnp.sum(jnp.where(low, 0.0, u), -1, keepdims=True)
    return jnp.where(low, first, second) * (1.0 / 64)


def head_norm(u, gain):
    return u * lax.rsqrt(head_mean(u * u) + EPS) * gain


def head_norm_back(u, gain, grads):
    inv = lax.rsqrt(head_mean(u * u) + EPS)
    scaled = grads * gain
    back = inv * (scaled - u * (inv * inv) * head_mean(scaled * u))
    return back, grads * u * inv


def row_inverse(u):
    return lax.rsqrt(jnp.mean(u * u, -1, keepdims=True) + EPS)


def row_norm_back(u, gain, grads):
    inv = row_inverse(u)
    scaled = grads * gain
    back = inv * (scaled - u * (inv * inv) * jnp.mean(scaled * u, -1, keepdims=True))
    return back, grads * u * inv


def to_diagonal(part, kv, ref):
    low = lanes((64, 128)) < 64
    for s in range(2):
        for h in range(2):
            a = part[(s * 2 + h) * 64 : (s * 2 + h + 1) * 64]
            b = pltpu.roll(a, 64, 1)
            first, second = (a, b) if kv == 0 else (b, a)
            keep = low if kv == 0 else jnp.logical_not(low)
            at = h * 256 + kv * 128
            ref[s, at : at + 64, :] = jnp.where(keep, first, 0.0).astype(ref.dtype)
            ref[s, at + 64 : at + 128, :] = jnp.where(keep, second, 0.0).astype(ref.dtype)


def from_diagonal(rows, kv):
    low = lanes((64, 128)) < 64
    a = rows[kv * 128 : kv * 128 + 64]
    b = rows[kv * 128 + 64 : kv * 128 + 128]
    if kv == 0:
        return jnp.where(low, a, pltpu.roll(b, 64, 1))
    return jnp.where(low, pltpu.roll(a, 64, 1), b)


def kernel(
    x, ng, wq_in, wk, wv, qg, kg, wo_in, pg, wg_in, wu_in, wd_in, gy_in, cr, sr, cb, sb,
    mixed_out, xgrad_out, ng_out, wq_out, wk_out, wv_out, qg_out, kg_out, wo_out, pg_out, gate_out, up_out, down_out,
    wg, wu, wd, wq, gy, wo_all, nrm, kv_all, kp, qp, ct, st_, qbd, dobd, ot, sums, stats, att_all,
    mid, post, hid, gg, ug, pp, ppb, mpb, ipb, xr, ml, mgr, mixed_s, xg_s, dq, dql, kvl,
    g1, r1, ra1, rb1, dkv, r0, ra0, rb0, g2, r2, ra2, rb2, g3, r3, ra3, rb3, gv, gr,
    loc, kss, krs, xss, xrs, yss, yrs, wss, wrs, s1, q1, s0, q0, s2, q2, s3, q3, bs0, bq0, gss, grs,
):
    c = lax.axis_index("ctx")
    t = lax.axis_index("tp")
    cy = lax.div(c, 8)
    cz = lax.rem(lax.div(c, 2), 4)
    ck = lax.rem(c, 2)
    sib = 1 - ck

    def off(v, d):
        return lax.rem(v + d + 4, 4)

    def at_y(d):
        return ((off(cy, d) * 4 + cz) * 2 + ck, t)

    def at_z(d):
        return ((cy * 4 + off(cz, d)) * 2 + ck, t)

    def at_x(d):
        return (c, off(t, d))

    def at_ky(d):
        return ((off(cy, d) * 4 + cz) * 2 + sib, t)

    at_k = at_ky(0)
    order = (1, 3, 2)

    barrier = pltpu.get_barrier_semaphore()
    for d in order:
        for peer in (at_x(d), at_y(d), at_z(d)):
            pl.semaphore_signal(barrier, inc=1, device_id=peer, device_id_type=MESH)
    for d in range(4):
        pl.semaphore_signal(barrier, inc=1, device_id=at_ky(d), device_id_type=MESH)

    locals_ = []
    for n, (src, dst) in enumerate(
        ((wo_in, wo_all.at[t]), (wq_in, wq), (wg_in, wg), (wu_in, wu), (wd_in, wd), (gy_in, gy))
    ):
        cp = pltpu.make_async_copy(src, dst, loc.at[n])
        cp.start()
        locals_.append(cp)

    sent = []

    def remote_copy(src, dst, ssem, rsem, peer):
        return pltpu.make_async_remote_copy(
            src_ref=src, dst_ref=dst, send_sem=ssem, recv_sem=rsem, device_id=peer, device_id_type=MESH
        )

    def remote(src, dst, ssem, rsem, peer):
        cp = remote_copy(src, dst, ssem, rsem, peer)
        cp.start()
        sent.append(cp)
        return cp

    xf = x[...].astype(F32)
    nrm[...] = (xf * row_inverse(xf) * ng[...]).astype(BF)
    lane64 = lanes((64, 128))
    sign = jnp.where(lane64 % 64 < 32, -1.0, 1.0)
    for h in range(2):
        place = c if h == 0 else 63 - c
        cos_b, sin_b = cb[pl.ds(place, 1), :], sb[pl.ds(place, 1), :]
        cos_h = cos_b * cr[...] - sin_b * sr[...]
        sin_h = (sin_b * cr[...] + cos_b * sr[...]) * sign
        for s in range(2):
            ct[pl.ds((s * 2 + h) * 64, 64), :] = cos_h
            st_[pl.ds((s * 2 + h) * 64, 64), :] = sin_h

    def rotate(u):
        return u * ct[...] + swap_halves(u) * st_[...]

    def rotate_back(u):
        return u * ct[...] - swap_halves(u) * st_[...]

    key_gain = jnp.concatenate([kg[...], kg[...]], 1)
    query_gain = jnp.concatenate([qg[...], qg[...]], 1)
    kproj = dot(nrm[...], wk[...])
    kp[...] = kproj
    kv_all[0, c] = rotate(head_norm(kproj, key_gain)).astype(BF)
    kv_all[1, c] = dot(nrm[...], wv[...]).astype(BF)

    pl.semaphore_wait(barrier, 13)

    arrive = {}

    def pass_on(kind, dy, dz, axis, d):
        source = (off(cy, -dy) * 4 + off(cz, -dz)) * 2 + ck
        if axis == "y":
            key, peer = (dy + d, dz, 0), at_y(d)
        elif axis == "z":
            key, peer = (dy, dz + d, 0), at_z(d)
        else:
            key, peer = (dy, dz, 1), at_k
        n = (key[0] * 4 + key[1]) * 2 + key[2]
        ref = kv_all.at[kind, source]
        arrive[kind, key] = remote(ref, ref, kss.at[kind, n], krs.at[kind, n], peer)

    for d in order:
        pass_on(0, 0, 0, "y", d)
        pass_on(1, 0, 0, "z", d)
    for kind in range(2):
        pass_on(kind, 0, 0, "k", 1)
    for d in order:
        pass_on(0, 0, 0, "z", d)
        pass_on(1, 0, 0, "y", d)

    locals_[0].wait()
    def out_half(n):
        return wo_all.at[n, pl.ds(pl.multiple_of(ck * 128, 128), 128)]

    wo_c = [remote(out_half(t), out_half(t), xss.at[8, d - 1], xrs.at[8, d - 1], at_x(d)) for d in order]

    locals_[1].wait()
    for kv in range(2):
        proj = dot(nrm[...], wq[:, kv * 128 : (kv + 1) * 128])
        qp[kv] = proj
        to_diagonal(rotate(head_norm(proj, query_gain)).astype(BF).astype(F32) * 0.125, kv, qbd)

    def seq_rows(s, kh):
        return pl.ds(pl.multiple_of((s * 2 + kh) * 64, 64), 64)

    def chunk(kind, j, s, kh):
        return kv_all[kind, pl.ds(j * 8, 8), seq_rows(s, kh), :].reshape(512, 128)

    def visible_front(width):
        keys = lax.broadcasted_iota(jnp.int32, (512, width), 0)
        lane = lax.broadcasted_iota(jnp.int32, (512, width), 1)
        return (keys <= lax.rem(c, 8) * 64 + lane % 64) | (lane >= 256)

    def visible_back():
        keys = lax.broadcasted_iota(jnp.int32, (512, 256), 0)
        lane = lax.broadcasted_iota(jnp.int32, (512, 256), 1)
        return keys % 64 - 64 * (keys // 64) <= lane % 64 - 64 * lax.rem(c, 8)

    def tile(s, j, kh, h, seen):
        p = jnp.exp(dot(chunk(0, j, s, kh), qbd[s, pl.ds(pl.multiple_of(h * 256, 256), 256), :], NT))
        if seen is not None:
            p = jnp.where(seen, p, 0.0)
        sums[s, h, 0:1, :] += jnp.sum(p, 0, keepdims=True)
        ot[s, h] += dot(chunk(1, j, s, kh), p.astype(BF), TN)

    def attend(s, dy):
        j = off(cy, -dy)
        if dy == 0:
            tile(s, j, 0, 0, visible_front(256))
            tile(s, j, 0, 1, None)
            tile(s, j, 1, 1, visible_back())
        else:
            later = jnp.where(j > cy, 1, 0)
            tile(s, j, 0, 1, None)
            tile(s, j, later, later, None)

    def await_sibling(dy):
        for kind in range(2):
            for dz in range(4):
                arrive[kind, (dy, dz, 1)].wait_recv()

    ot[...] = jnp.zeros_like(ot)
    sums[...] = jnp.zeros_like(sums)
    for d in order:
        arrive[0, (d, 0, 0)].wait_recv()
        for e in order:
            pass_on(0, d, 0, "z", e)
        pass_on(0, d, 0, "k", 1)
    for d in order:
        arrive[1, (0, d, 0)].wait_recv()
        pass_on(1, 0, d, "k", 1)
    for d in order:
        for e in order:
            pass_on(1, 0, e, "y", d)

    def pass_row(dy):
        for e in order:
            arrive[0, (dy, e, 0)].wait_recv()
            pass_on(0, dy, e, "k", 1)
        if dy > 0:
            for e in (0,) + order:
                arrive[1, (dy, e, 0)].wait_recv()
                pass_on(1, dy, e, "k", 1)

    pass_row(0)
    await_sibling(0)
    for s in range(2):
        attend(s, 0)
    pass_row(1)
    pass_row(3)
    await_sibling(1)
    for s in range(2):
        attend(s, 1)
    wo_k = []
    for d, cp in zip(order, wo_c):
        cp.wait_recv()
        half = out_half(off(t, -d))
        wo_k.append(remote(half, half, wss.at[d - 1], wrs.at[d - 1], at_k))
    pass_row(2)
    await_sibling(3)
    for s in range(2):
        attend(s, 3)
    await_sibling(2)
    att_c = []
    for s in range(2):
        attend(s, 2)
        for h in range(2):
            l = sums[s, h, 0:1, :]
            o = ot[s, h] / l
            ot[s, h] = o
            stats[s, 0:1, h * 256 : (h + 1) * 256] = jnp.log(l)
            rows = o.T
            for kv in range(2):
                att_all[t, pl.ds((s * 2 + h) * 64, 64), kv * 128 : (kv + 1) * 128] = from_diagonal(
                    rows, kv
                ).astype(BF)
        part = att_all.at[t, pl.ds(s * 128, 128)]
        att_c += [remote(part, part, xss.at[6 + s, d - 1], xrs.at[6 + s, d - 1], at_x(d)) for d in order]

    for cp in locals_[2:]:
        cp.wait()
    for cp in wo_k:
        cp.wait_recv()
    for cp in att_c:
        cp.wait_recv()

    branch = dot(att_all[0], wo_all[0])
    for n in range(1, 4):
        branch = branch + dot(att_all[n], wo_all[n])
    mid[...] = x[...].astype(F32) + branch
    post[...] = (mid[...] * row_inverse(mid[...]) * pg[...]).astype(BF)

    def mlp_step(n, _):
        cols = pl.ds(pl.multiple_of(n * 384, 128), 384)
        g = dot(post[...], wg[:, cols])
        u = dot(post[...], wu[:, cols])
        hgrad = dot(gy[...], wd[cols, :], NT)
        sg = 1.0 / (1.0 + jnp.exp(-g))
        silu = g * sg
        hid[:, cols] = (silu * u).astype(BF)
        gg[:, cols] = (hgrad * u * sg * (1.0 + g * (1.0 - sg))).astype(BF)
        ug[:, cols] = (hgrad * silu).astype(BF)
        return 0

    lax.fori_loop(0, 3, mlp_step, 0)

    def rows_of(n):
        return pl.ds(pl.multiple_of(n * 64, 64), 64)

    def piece(n, p):
        return pl.ds(pl.multiple_of(n * 64 + p * 32, 32), 32)

    def scatter_x(src, n, p, d):
        return remote(
            src.at[piece(off(t, d), p)], xr.at[n, d - 1, pl.ds(p * 32, 32)], xss.at[n * 2 + p, d - 1],
            xrs.at[n * 2 + p, d - 1], at_x(d),
        )

    def collect_x(src, n, p, copies):
        whole = src[piece(t, p), :].astype(F32)
        for cp in copies:
            cp.wait_recv()
        for d in range(3):
            whole = whole + xr[n, d, p * 32 : p * 32 + 32, :].astype(F32)
        return whole

    def spread_x(buf, n, p):
        ref = buf.at[piece(t, p)]
        return [remote(ref, ref, yss.at[n * 2 + p, d - 1], yrs.at[n * 2 + p, d - 1], at_x(d)) for d in order]

    post_c = [[], []]
    for pair in ((2, 1), (3, 0)):
        lhs = [jnp.concatenate([ref[rows_of(off(t, d)), :] for d in pair], 0) for ref in (gg, ug)]
        part = (dot(lhs[0], wg[...], NT) + dot(lhs[1], wu[...], NT)).astype(BF)
        for n, d in enumerate(pair):
            ppb[rows_of(off(t, d)), :] = part[n * 64 : n * 64 + 64]
        for p in range(2):
            for d in pair:
                if d > 0:
                    post_c[p].append(scatter_x(ppb, 0, p, d))
    mpb[...] = dot(hid[...], wd[...]).astype(BF)

    def core_stage(g, r, ss, qs, y):
        return remote(g.at[y, :, sib], r.at[y], ss.at[y], qs.at[y], at_k)

    def core_sum(g, r, y, copy):
        copy.wait_recv()

        def add(z, _):
            r[y, z] = (g[y, z, ck].astype(F32) + r[y, z].astype(F32)).astype(BF)
            return 0

        lax.fori_loop(0, 4, add, 0)

    def first_stage(r, ra, ss, qs):
        out = []
        for d in order:
            out.append(remote(r.at[off(cy, d), :, 0], ra.at[0, d - 1], ss.at[3 + d], qs.at[3 + d], at_y(d)))
            out.append(remote(r.at[:, off(cz, d), 1], ra.at[1, d - 1], ss.at[6 + d], qs.at[6 + d], at_z(d)))
        return out

    def first_sum(r, ra, copies):
        for cp in copies:
            cp.wait_recv()

        def add(n, _):
            for half, at in ((0, (cy, n)), (1, (n, cz))):
                total = r[at[0], at[1], half].astype(F32)
                for d in range(3):
                    total = total + ra[half, d, n].astype(F32)
                r[at[0], at[1], half] = total.astype(BF)
            return 0

        lax.fori_loop(0, 4, add, 0)

    def second_stage(r, rb, ss, qs):
        out = []
        for d in order:
            out.append(remote(r.at[cy, off(cz, d), 0], rb.at[0, d - 1], ss.at[9 + d], qs.at[9 + d], at_z(d)))
            out.append(remote(r.at[off(cy, d), cz, 1], rb.at[1, d - 1], ss.at[12 + d], qs.at[12 + d], at_y(d)))
        return out

    def second_sum(r, rb, copies):
        for cp in copies:
            cp.wait_recv()
        out = []
        for half in range(2):
            total = r[cy, cz, half].astype(F32)
            for d in range(3):
                total = total + rb[half, d].astype(F32)
            out.append(total)
        return out

    def weight_part(g, lhs, rhs, at, y):
        width = rhs.shape[1]
        part = dot(lhs[:, y * 256 : (y + 1) * 256], rhs[...], TN).astype(BF)
        g[y, :, :, :, :, at : at + width] = part.reshape(4, 2, 2, 16, width)

    core1 = []
    for y in range(4):
        weight_part(g1, post, gg, 0, y)
        weight_part(g1, post, ug, FF, y)
        core1.append(core_stage(g1, r1, s1, q1, y))

    ml_c = []
    for p in range(2):
        post_grad = collect_x(ppb, 0, p, post_c[p])
        back, term = row_norm_back(mid[piece(t, p), :], pg[...], post_grad)
        mgr[p * 32 : p * 32 + 32, :] = gy[piece(t, p), :].astype(F32) + back
        ml[piece(t, p), :] = mgr[p * 32 : p * 32 + 32, :].astype(BF)
        ml_c += spread_x(ml, 0, p)
        gain = jnp.sum(term, 0, keepdims=True)
        post_gain_term = gain if p == 0 else post_gain_term + gain

    for y in range(4):
        core_sum(g1, r1, y, core1[y])
    first1 = first_stage(r1, ra1, s1, q1)

    for y in range(4):
        weight_part(g3, gy, hid, 0, y)
    for cp in ml_c:
        cp.wait_recv()
    mlp_c = [[scatter_x(mpb, 1, p, d) for d in order] for p in range(2)]

    ag = dot(ml[...], wo_all[t], NT).astype(BF).astype(F32)
    for kv in range(2):
        to_diagonal(ag[:, kv * 128 : (kv + 1) * 128], kv, dobd)
    for s in range(2):
        for h in range(2):
            at = slice(h * 256, (h + 1) * 256)
            stats[s, 1:2, at] = jnp.sum(dobd[s, at, :].astype(F32).T * ot[s, h], 0, keepdims=True)
    dq[...] = jnp.zeros_like(dq)

    def back_step(j, s, kh, first, seen):
        at = slice(first, 512)
        kc, vc = chunk(0, j, s, kh), chunk(1, j, s, kh)
        q, do = qbd[s, at, :], dobd[s, at, :]
        p = jnp.exp(dot(kc, q, NT) - stats[s, 0:1, at])
        if seen is not None:
            p = jnp.where(seen, p, 0.0)
        ds = (p * (dot(vc, do, NT) - stats[s, 1:2, at])).astype(BF)
        where = pl.ds((s * 2 + kh) * 64, 64)
        dkv[j, :, :, 1, where, :] = dot(p.astype(BF), do).astype(BF).reshape(4, 2, 64, 128)
        dkv[j, :, :, 0, where, :] = dot(ds, q).astype(BF).reshape(4, 2, 64, 128)
        dq[s, at, :] += dot(ds, kc, TN)

    def key_core(j):
        return remote_copy(dkv.at[j, :, sib], r0.at[j], s0.at[j], q0.at[j], at_k)

    def key_along_y(j):
        d = lax.rem(j - cy + 4, 4)
        peer = ((j * 4 + cz) * 2 + ck, t)
        return remote_copy(r0.at[j, :, 0], ra0.at[0, d - 1], s0.at[3 + d], q0.at[3 + d], peer)

    def key_along_z(j):
        return [
            remote_copy(r0.at[j, off(cz, d), 1], ra0.at[1, d - 1, j], bs0.at[d - 1, j], bq0.at[d - 1, j], at_z(d))
            for d in order
        ]

    def key_step(n, _):
        j = off(cy, n + 1)

        @pl.when(n < 4)
        def _():
            @pl.when(j < cy)
            def _():
                for s in range(2):
                    back_step(j, s, 0, 0, None)
                    for kind in range(2):
                        dkv[j, :, :, kind, pl.ds((s * 2 + 1) * 64, 64), :] = jnp.zeros((4, 2, 64, 128), BF)

            @pl.when(j > cy)
            def _():
                for s in range(2):
                    back_step(j, s, 0, 256, None)
                    back_step(j, s, 1, 256, None)

            @pl.when(j == cy)
            def _():
                for s in range(2):
                    back_step(j, s, 0, 0, visible_front(512))
                    back_step(j, s, 1, 256, visible_back())

            key_core(j).start()

        @pl.when(n > 0)
        def _():
            done = off(cy, n)
            core_sum(dkv, r0, done, key_core(done))

            @pl.when(n < 4)
            def _():
                key_along_y(done).start()

            for cp in key_along_z(done):
                cp.start()

        return 0

    lax.fori_loop(0, 5, key_step, 0)
    first0 = []
    for y in range(4):
        sent.append(key_core(y))
        first0 += key_along_z(y)
    for d in order:
        first0.append(
            remote_copy(r0.at[off(cy, d), :, 0], ra0.at[0, d - 1], s0.at[3 + d], q0.at[3 + d], at_y(d))
        )
    sent.extend(first0)

    query_gain_term = jnp.zeros((1, 128), F32)
    for kv in range(2):
        parts = [
            from_diagonal(dq[s, h * 256 : (h + 1) * 256, :], kv) for s in range(2) for h in range(2)
        ]
        grads = rotate_back(jnp.concatenate(parts, 0) * 0.125)
        back, term = head_norm_back(qp[kv], query_gain, grads)
        dql[:, kv * 128 : (kv + 1) * 128] = back.astype(BF)
        query_gain_term = query_gain_term + jnp.sum(term, 0, keepdims=True)

    mixed_c = []
    for p in range(2):
        mixed_s[piece(t, p), :] = (mid[piece(t, p), :] + collect_x(mpb, 1, p, mlp_c[p])).astype(BF)
        mixed_c += spread_x(mixed_s, 1, p)

    first_sum(r0, ra0, first0)
    second0 = second_stage(r0, rb0, s0, q0)
    first_sum(r1, ra1, first1)
    second1 = second_stage(r1, rb1, s1, q1)

    core3 = []
    for y in range(4):
        weight_part(g3, ml, att_all.at[t], FF, y)
        weight_part(g3, nrm, dql, FF + 256, y)
        core3.append(core_stage(g3, r3, s3, q3, y))
    pp[...] = dot(dql[...], wq[...], NT)

    key_grad, value_grad = second_sum(r0, rb0, second0)
    back, term = head_norm_back(kp[...], key_gain, rotate_back(key_grad))
    kvl[:, 0:128] = back.astype(BF)
    kvl[:, 128:256] = value_grad.astype(BF)
    key_gain_term = jnp.sum(term, 0, keepdims=True)

    ipb[...] = (pp[...] + dot(kvl[:, 0:128], wk[...], NT) + dot(kvl[:, 128:256], wv[...], NT)).astype(BF)
    in_c = [[scatter_x(ipb, 2, p, d) for d in order] for p in range(2)]
    for y in range(4):
        core_sum(g3, r3, y, core3[y])
    first3 = first_stage(r3, ra3, s3, q3)
    for y in range(4):
        weight_part(g2, nrm, kvl, 0, y)
    core2 = [core_stage(g2, r2, s2, q2, y) for y in range(4)]

    for half, total in enumerate(second_sum(r1, rb1, second1)):
        rows = slice(half * 16, half * 16 + 16)
        gate_out[rows, :] = total[:, 0:FF]
        up_out[rows, :] = total[:, FF : 2 * FF]
    for y in range(4):
        core_sum(g2, r2, y, core2[y])
    first2 = first_stage(r2, ra2, s2, q2)

    bases = (0, 3, 10)

    def gain_stage(n, peers):
        return [
            remote(gv.at[n], gr.at[bases[n] + i], gss.at[bases[n] + i], grs.at[bases[n] + i], peer)
            for i, peer in enumerate(peers)
        ]

    def gain_sum(n, copies):
        whole = gv[n]
        for i, cp in enumerate(copies):
            cp.wait_recv()
            whole = whole + gr[bases[n] + i]
        return whole

    gv[0, 1:2, :] = post_gain_term
    gv[0, 2:8, :] = jnp.zeros((6, 1024), F32)
    gv[0, 2:3, 0:128] = query_gain_term + pltpu.roll(query_gain_term, 64, 1)
    gv[0, 3:4, 0:128] = key_gain_term + pltpu.roll(key_gain_term, 64, 1)
    xg_c = []
    for p in range(2):
        back, term = row_norm_back(
            x[piece(t, p), :].astype(F32), ng[...], collect_x(ipb, 2, p, in_c[p])
        )
        gain = jnp.sum(term, 0, keepdims=True)
        xg_s[piece(t, p), :] = (mgr[p * 32 : p * 32 + 32, :] + back).astype(BF)
        if p == 0:
            norm_gain_term = gain
        else:
            gv[0, 0:1, :] = norm_gain_term + gain
            gain_c = gain_stage(0, [at_x(d) for d in order])
        xg_c += spread_x(xg_s, 2, p)
    gv[1] = gain_sum(0, gain_c)
    gain_c = gain_stage(1, [at_k] + [at_y(d) for d in order] + [at_ky(d) for d in order])
    first_sum(r2, ra2, first2)
    second2 = second_stage(r2, rb2, s2, q2)
    first_sum(r3, ra3, first3)
    second3 = second_stage(r3, rb3, s3, q3)
    gv[2] = gain_sum(1, gain_c)
    gain_c = gain_stage(2, [at_z(d) for d in order])
    for cp in mixed_c:
        cp.wait_recv()
    mixed_out[...] = mixed_s[...]
    for half, total in enumerate(second_sum(r3, rb3, second3)):
        rows = slice(half * 16, half * 16 + 16)
        down_out[rows, :] = total[:, 0:FF]
        wo_out[rows, :] = total[:, FF : FF + 256]
        wq_out[rows, :] = total[:, FF + 256 : FF + 512]
    for half, total in enumerate(second_sum(r2, rb2, second2)):
        rows = slice(half * 16, half * 16 + 16)
        wk_out[rows, :] = total[:, 0:128]
        wv_out[rows, :] = total[:, 128:256]
    gains = gain_sum(2, gain_c)
    for cp in xg_c:
        cp.wait_recv()
    xgrad_out[...] = xg_s[...]
    ng_out[...] = gains[0:1, :]
    pg_out[...] = gains[1:2, :]
    qg_out[...] = gains[2:3, 0:64]
    kg_out[...] = gains[3:4, 0:64]
    for cp in sent:
        cp.wait_send()


def hand_out(*refs):
    count = len(refs) // 2
    for source, target in zip(refs[:count], refs[count:]):
        target[...] = source[...]


def on_device(
    tokens, norm_gain, query_weight, key_weight, value_weight, query_gain, key_gain, out_weight,
    post_gain, gate_weight, up_weight, down_weight, cotangent,
):
    x = tokens.reshape(256, 1024)
    gy = cotangent.reshape(256, 1024)
    tables = [jnp.asarray(a) for a in rope_constants()]
    cr, sr, cb, sb = tables
    vm = pl.BlockSpec(memory_space=pltpu.VMEM)
    hbm = pl.BlockSpec(memory_space=pl.ANY)
    V = pltpu.VMEM
    sem = lambda *s: pltpu.SemaphoreType.DMA(s)

    def ring(rows, width):
        return [V(lead + (rows, width), BF) for lead in ((4, 4, 2, 2), (4, 4, 2), (2, 3, 4), (2, 3))]

    scratch = [
        V((1024, FF), BF), V((1024, FF), BF), V((FF, 1024), BF),
        V((1024, 256), BF), V((256, 1024), BF), V((4, 256, 1024), BF),
        V((256, 1024), BF), V((2, 32, 256, 128), BF), V((256, 128), F32), V((2, 256, 128), F32),
        V((256, 128), F32), V((256, 128), F32), V((2, 512, 128), BF), V((2, 512, 128), BF),
        V((2, 2, 128, 256), F32), V((2, 2, 8, 256), F32), V((2, 8, 512), F32), V((4, 256, 256), BF),
        V((256, 1024), F32), V((256, 1024), BF), V((256, FF), BF), V((256, FF), BF), V((256, FF), BF),
        V((256, 1024), F32), V((256, 1024), BF), V((256, 1024), BF), V((256, 1024), BF),
        V((3, 3, 64, 1024), BF),
        V((256, 1024), BF), V((64, 1024), F32), V((256, 1024), BF), V((256, 1024), BF),
        V((2, 512, 128), F32), V((256, 256), BF), V((256, 256), BF),
        *ring(16, G1X),
        *ring(256, 128),
        *ring(16, G2X),
        *ring(16, G3X),
        V((3, 8, 1024), F32), V((13, 8, 1024), F32),
        sem(6), sem(2, 32), sem(2, 32), sem(9, 3), sem(9, 3), sem(6, 3), sem(6, 3), sem(3), sem(3),
        *[sem(16)] * 8, sem(3, 4), sem(3, 4), sem(13), sem(13),
    ]
    shape = jax.ShapeDtypeStruct
    outs = [
        shape((256, 1024), BF), shape((256, 1024), BF), shape((1, 1024), F32),
        shape((32, 256), F32), shape((32, 128), F32), shape((32, 128), F32),
        shape((1, 64), F32), shape((1, 64), F32), shape((32, 256), F32), shape((1, 1024), F32),
        shape((32, FF), F32), shape((32, FF), F32), shape((32, FF), F32),
    ]
    results = pl.pallas_call(
        kernel,
        name="block",
        out_shape=outs,
        in_specs=[vm] * 2 + [hbm] + [vm] * 4 + [hbm] + [vm] + [hbm] * 4 + [vm] * 4,
        out_specs=[vm] * 13,
        scratch_shapes=scratch,
        compiler_params=pltpu.CompilerParams(
            collective_id=0, has_side_effects=True, vmem_limit_bytes=63 * 2**20
        ),
    )(
        x, norm_gain.reshape(1, 1024), query_weight, key_weight, value_weight,
        query_gain.reshape(1, 64), key_gain.reshape(1, 64),
        out_weight, post_gain.reshape(1, 1024), gate_weight, up_weight, down_weight, gy, cr, sr, cb, sb,
    )
    results = pl.pallas_call(
        hand_out,
        name="hand_out",
        out_shape=outs,
        in_specs=[vm] * 13,
        out_specs=[vm] * 13,
    )(*results)
    mixed, xgrad, ng, wq, wk, wv, qg, kg, wo, pg, gate, up, down = results
    place = (2, 2, 1, 64, 1024)
    return (
        mixed.reshape(place), xgrad.reshape(place), ng.reshape(1024), wq, wk, wv, qg.reshape(64), kg.reshape(64),
        wo.T, pg.reshape(1024), gate, up, down.T,
    )


def solution(mesh):
    tok = P(None, None, "ctx", None, None)
    col = P(None, "tp")
    row = P("tp", None)
    return jax.shard_map(
        on_device,
        mesh=mesh,
        in_specs=(tok, P(), col, col, col, P(), P(), row, P(), col, col, row, tok),
        out_specs=(
            tok, tok, P(), P("ctx", "tp"), P("ctx", "tp"), P("ctx", "tp"), P(), P(), P("tp", "ctx"), P(),
            P("ctx", "tp"), P("ctx", "tp"), P("tp", "ctx"),
        ),
        check_vma=False,
    )
```

```python
import jax
import jax.numpy as jnp
import numpy as np
from jax import lax
from jax.experimental import pallas as pl
from jax.experimental.pallas import tpu as pltpu
from jax.sharding import PartitionSpec as P

HD = 64
EPS = 1e-05
ROPE_BASE = 1000000.0
BF = jnp.bfloat16
F32 = jnp.float32
MESH = pl.DeviceIdType.MESH
FF = 1152
G1X = 2 * FF
G2X = 256
G3X = FF + 512

NN = (((1,), (0,)), ((), ()))
NT = (((1,), (1,)), ((), ()))
TN = (((0,), (0,)), ((), ()))


def dot(a, b, dims=NN):
    return lax.dot_general(a, b, dims, preferred_element_type=F32)


def rope_constants():
    freq = ROPE_BASE ** (-np.arange(0, HD, 2) / HD)
    freq = np.tile(freq, 4)[None, :]
    rows = np.arange(64)[:, None] * freq
    blocks = np.arange(64)[:, None] * 64.0 * freq
    return [f(a).astype(np.float32) for a in (rows, blocks) for f in (np.cos, np.sin)]


def lanes(shape):
    return lax.broadcasted_iota(jnp.int32, shape, len(shape) - 1)


def swap_halves(u):
    return jnp.where(lanes(u.shape) % 64 < 32, pltpu.roll(u, 96, 1), pltpu.roll(u, 32, 1))


def head_mean(u):
    low = lanes(u.shape) < 64
    first = jnp.sum(jnp.where(low, u, 0.0), -1, keepdims=True)
    second = jnp.sum(jnp.where(low, 0.0, u), -1, keepdims=True)
    return jnp.where(low, first, second) * (1.0 / 64)


def head_norm(u, gain):
    return u * lax.rsqrt(head_mean(u * u) + EPS) * gain


def head_norm_back(u, gain, grads):
    inv = lax.rsqrt(head_mean(u * u) + EPS)
    scaled = grads * gain
    back = inv * (scaled - u * (inv * inv) * head_mean(scaled * u))
    return back, grads * u * inv


def row_inverse(u):
    return lax.rsqrt(jnp.mean(u * u, -1, keepdims=True) + EPS)


def row_norm_back(u, gain, grads):
    inv = row_inverse(u)
    scaled = grads * gain
    back = inv * (scaled - u * (inv * inv) * jnp.mean(scaled * u, -1, keepdims=True))
    return back, grads * u * inv


def to_diagonal(part, kv, ref):
    low = lanes((64, 128)) < 64
    for s in range(2):
        for h in range(2):
            a = part[(s * 2 + h) * 64 : (s * 2 + h + 1) * 64]
            b = pltpu.roll(a, 64, 1)
            first, second = (a, b) if kv == 0 else (b, a)
            keep = low if kv == 0 else jnp.logical_not(low)
            at = h * 256 + kv * 128
            ref[s, at : at + 64, :] = jnp.where(keep, first, 0.0).astype(ref.dtype)
            ref[s, at + 64 : at + 128, :] = jnp.where(keep, second, 0.0).astype(ref.dtype)


def from_diagonal(rows, kv):
    low = lanes((64, 128)) < 64
    a = rows[kv * 128 : kv * 128 + 64]
    b = rows[kv * 128 + 64 : kv * 128 + 128]
    if kv == 0:
        return jnp.where(low, a, pltpu.roll(b, 64, 1))
    return jnp.where(low, pltpu.roll(a, 64, 1), b)


def kernel(
    x, ng, wq_in, wk, wv, qg, kg, wo_in, pg, wg_in, wu_in, wd_in, gy_in, cr, sr, cb, sb,
    mixed_out, xgrad_out, ng_out, wq_out, wk_out, wv_out, qg_out, kg_out, wo_out, pg_out, gate_out, up_out, down_out,
    wg, wu, wd, wq, gy, wo_all, nrm, kv_all, kp, qp, ct, st_, qbd, dobd, ot, sums, stats, att_all,
    mid, post, hid, gg, ug, pp, ppb, mpb, ipb, xr, ml, mgr, mixed_s, xg_s, dq, dql, kvl,
    g1, r1, ra1, rb1, dkv, r0, ra0, rb0, g2, r2, ra2, rb2, g3, r3, ra3, rb3, gv, gr,
    loc, kss, krs, xss, xrs, yss, yrs, wss, wrs, s1, q1, s0, q0, s2, q2, s3, q3, bs0, bq0, gss, grs,
):
    c = lax.axis_index("ctx")
    t = lax.axis_index("tp")
    cy = lax.div(c, 8)
    cz = lax.rem(lax.div(c, 2), 4)
    ck = lax.rem(c, 2)
    sib = 1 - ck

    def off(v, d):
        return lax.rem(v + d + 4, 4)

    def at_y(d):
        return ((off(cy, d) * 4 + cz) * 2 + ck, t)

    def at_z(d):
        return ((cy * 4 + off(cz, d)) * 2 + ck, t)

    def at_x(d):
        return (c, off(t, d))

    def at_ky(d):
        return ((off(cy, d) * 4 + cz) * 2 + sib, t)

    at_k = at_ky(0)
    order = (1, 3, 2)

    barrier = pltpu.get_barrier_semaphore()
    for d in order:
        for peer in (at_x(d), at_y(d), at_z(d)):
            pl.semaphore_signal(barrier, inc=1, device_id=peer, device_id_type=MESH)
    for d in range(4):
        pl.semaphore_signal(barrier, inc=1, device_id=at_ky(d), device_id_type=MESH)

    locals_ = []
    for n, (src, dst) in enumerate(
        ((wo_in, wo_all.at[t]), (wq_in, wq), (wg_in, wg), (wu_in, wu), (wd_in, wd), (gy_in, gy))
    ):
        cp = pltpu.make_async_copy(src, dst, loc.at[n])
        cp.start()
        locals_.append(cp)

    sent = []

    def remote_copy(src, dst, ssem, rsem, peer):
        return pltpu.make_async_remote_copy(
            src_ref=src, dst_ref=dst, send_sem=ssem, recv_sem=rsem, device_id=peer, device_id_type=MESH
        )

    def remote(src, dst, ssem, rsem, peer):
        cp = remote_copy(src, dst, ssem, rsem, peer)
        cp.start()
        sent.append(cp)
        return cp

    xf = x[...].astype(F32)
    nrm[...] = (xf * row_inverse(xf) * ng[...]).astype(BF)
    lane64 = lanes((64, 128))
    sign = jnp.where(lane64 % 64 < 32, -1.0, 1.0)
    for h in range(2):
        place = c if h == 0 else 63 - c
        cos_b, sin_b = cb[pl.ds(place, 1), :], sb[pl.ds(place, 1), :]
        cos_h = cos_b * cr[...] - sin_b * sr[...]
        sin_h = (sin_b * cr[...] + cos_b * sr[...]) * sign
        for s in range(2):
            ct[pl.ds((s * 2 + h) * 64, 64), :] = cos_h
            st_[pl.ds((s * 2 + h) * 64, 64), :] = sin_h

    def rotate(u):
        return u * ct[...] + swap_halves(u) * st_[...]

    def rotate_back(u):
        return u * ct[...] - swap_halves(u) * st_[...]

    key_gain = jnp.concatenate([kg[...], kg[...]], 1)
    query_gain = jnp.concatenate([qg[...], qg[...]], 1)
    kproj = dot(nrm[...], wk[...])
    kp[...] = kproj
    kv_all[0, c] = rotate(head_norm(kproj, key_gain)).astype(BF)
    kv_all[1, c] = dot(nrm[...], wv[...]).astype(BF)

    pl.semaphore_wait(barrier, 13)

    arrive = {}

    def pass_on(kind, dy, dz, axis, d):
        source = (off(cy, -dy) * 4 + off(cz, -dz)) * 2 + ck
        if axis == "y":
            key, peer = (dy + d, dz, 0), at_y(d)
        elif axis == "z":
            key, peer = (dy, dz + d, 0), at_z(d)
        else:
            key, peer = (dy, dz, 1), at_k
        n = (key[0] * 4 + key[1]) * 2 + key[2]
        ref = kv_all.at[kind, source]
        arrive[kind, key] = remote(ref, ref, kss.at[kind, n], krs.at[kind, n], peer)

    for d in order:
        pass_on(0, 0, 0, "y", d)
        pass_on(1, 0, 0, "z", d)
    for kind in range(2):
        pass_on(kind, 0, 0, "k", 1)
    for d in order:
        pass_on(0, 0, 0, "z", d)
        pass_on(1, 0, 0, "y", d)

    locals_[0].wait()
    def out_half(n):
        return wo_all.at[n, pl.ds(pl.multiple_of(ck * 128, 128), 128)]

    wo_c = [remote(out_half(t), out_half(t), xss.at[8, d - 1], xrs.at[8, d - 1], at_x(d)) for d in order]

    locals_[1].wait()
    for kv in range(2):
        proj = dot(nrm[...], wq[:, kv * 128 : (kv + 1) * 128])
        qp[kv] = proj
        to_diagonal(rotate(head_norm(proj, query_gain)).astype(BF).astype(F32) * 0.125, kv, qbd)

    def seq_rows(s, kh):
        return pl.ds(pl.multiple_of((s * 2 + kh) * 64, 64), 64)

    def chunk(kind, j, s, kh):
        return kv_all[kind, pl.ds(j * 8, 8), seq_rows(s, kh), :].reshape(512, 128)

    def visible_front(width):
        keys = lax.broadcasted_iota(jnp.int32, (512, width), 0)
        lane = lax.broadcasted_iota(jnp.int32, (512, width), 1)
        return (keys <= lax.rem(c, 8) * 64 + lane % 64) | (lane >= 256)

    def visible_back():
        keys = lax.broadcasted_iota(jnp.int32, (512, 256), 0)
        lane = lax.broadcasted_iota(jnp.int32, (512, 256), 1)
        return keys % 64 - 64 * (keys // 64) <= lane % 64 - 64 * lax.rem(c, 8)

    def tile(s, j, kh, h, seen):
        p = jnp.exp(dot(chunk(0, j, s, kh), qbd[s, pl.ds(pl.multiple_of(h * 256, 256), 256), :], NT))
        if seen is not None:
            p = jnp.where(seen, p, 0.0)
        sums[s, h, 0:1, :] += jnp.sum(p, 0, keepdims=True)
        ot[s, h] += dot(chunk(1, j, s, kh), p.astype(BF), TN)

    def attend(s, dy):
        j = off(cy, -dy)
        if dy == 0:
            tile(s, j, 0, 0, visible_front(256))
            tile(s, j, 0, 1, None)
            tile(s, j, 1, 1, visible_back())
        else:
            later = jnp.where(j > cy, 1, 0)
            tile(s, j, 0, 1, None)
            tile(s, j, later, later, None)

    def await_sibling(dy):
        for kind in range(2):
            for dz in range(4):
                arrive[kind, (dy, dz, 1)].wait_recv()

    ot[...] = jnp.zeros_like(ot)
    sums[...] = jnp.zeros_like(sums)
    for d in order:
        arrive[0, (d, 0, 0)].wait_recv()
        for e in order:
            pass_on(0, d, 0, "z", e)
        pass_on(0, d, 0, "k", 1)
    for d in order:
        arrive[1, (0, d, 0)].wait_recv()
        pass_on(1, 0, d, "k", 1)
    for d in order:
        for e in order:
            pass_on(1, 0, e, "y", d)

    def pass_row(dy):
        for e in order:
            arrive[0, (dy, e, 0)].wait_recv()
            pass_on(0, dy, e, "k", 1)
        if dy > 0:
            for e in (0,) + order:
                arrive[1, (dy, e, 0)].wait_recv()
                pass_on(1, dy, e, "k", 1)

    pass_row(0)
    await_sibling(0)
    for s in range(2):
        attend(s, 0)
    pass_row(1)
    pass_row(3)
    await_sibling(1)
    for s in range(2):
        attend(s, 1)
    wo_k = []
    for d, cp in zip(order, wo_c):
        cp.wait_recv()
        half = out_half(off(t, -d))
        wo_k.append(remote(half, half, wss.at[d - 1], wrs.at[d - 1], at_k))
    pass_row(2)
    await_sibling(3)
    for s in range(2):
        attend(s, 3)
    await_sibling(2)
    att_c = []
    for s in range(2):
        attend(s, 2)
        for h in range(2):
            l = sums[s, h, 0:1, :]
            o = ot[s, h] / l
            ot[s, h] = o
            stats[s, 0:1, h * 256 : (h + 1) * 256] = jnp.log(l)
            rows = o.T
            for kv in range(2):
                att_all[t, pl.ds((s * 2 + h) * 64, 64), kv * 128 : (kv + 1) * 128] = from_diagonal(
                    rows, kv
                ).astype(BF)
        part = att_all.at[t, pl.ds(s * 128, 128)]
        att_c += [remote(part, part, xss.at[6 + s, d - 1], xrs.at[6 + s, d - 1], at_x(d)) for d in order]

    for cp in locals_[2:]:
        cp.wait()
    for cp in wo_k:
        cp.wait_recv()
    for cp in att_c:
        cp.wait_recv()

    branch = dot(att_all[0], wo_all[0])
    for n in range(1, 4):
        branch = branch + dot(att_all[n], wo_all[n])
    mid[...] = x[...].astype(F32) + branch
    post[...] = (mid[...] * row_inverse(mid[...]) * pg[...]).astype(BF)

    def mlp_step(n, _):
        cols = pl.ds(pl.multiple_of(n * 384, 128), 384)
        g = dot(post[...], wg[:, cols])
        u = dot(post[...], wu[:, cols])
        hgrad = dot(gy[...], wd[cols, :], NT)
        sg = 1.0 / (1.0 + jnp.exp(-g))
        silu = g * sg
        hid[:, cols] = (silu * u).astype(BF)
        gg[:, cols] = (hgrad * u * sg * (1.0 + g * (1.0 - sg))).astype(BF)
        ug[:, cols] = (hgrad * silu).astype(BF)
        return 0

    lax.fori_loop(0, 3, mlp_step, 0)

    def rows_of(n):
        return pl.ds(pl.multiple_of(n * 64, 64), 64)

    def piece(n, p):
        return pl.ds(pl.multiple_of(n * 64 + p * 32, 32), 32)

    def scatter_x(src, n, p, d):
        return remote(
            src.at[piece(off(t, d), p)], xr.at[n, d - 1, pl.ds(p * 32, 32)], xss.at[n * 2 + p, d - 1],
            xrs.at[n * 2 + p, d - 1], at_x(d),
        )

    def collect_x(src, n, p, copies):
        whole = src[piece(t, p), :].astype(F32)
        for cp in copies:
            cp.wait_recv()
        for d in range(3):
            whole = whole + xr[n, d, p * 32 : p * 32 + 32, :].astype(F32)
        return whole

    def spread_x(buf, n, p):
        ref = buf.at[piece(t, p)]
        return [remote(ref, ref, yss.at[n * 2 + p, d - 1], yrs.at[n * 2 + p, d - 1], at_x(d)) for d in order]

    post_c = [[], []]
    for pair in ((2, 1), (3, 0)):
        lhs = [jnp.concatenate([ref[rows_of(off(t, d)), :] for d in pair], 0) for ref in (gg, ug)]
        part = (dot(lhs[0], wg[...], NT) + dot(lhs[1], wu[...], NT)).astype(BF)
        for n, d in enumerate(pair):
            ppb[rows_of(off(t, d)), :] = part[n * 64 : n * 64 + 64]
        for p in range(2):
            for d in pair:
                if d > 0:
                    post_c[p].append(scatter_x(ppb, 0, p, d))
    mpb[...] = dot(hid[...], wd[...]).astype(BF)

    def core_stage(g, r, ss, qs, y):
        return remote(g.at[y, :, sib], r.at[y], ss.at[y], qs.at[y], at_k)

    def core_sum(g, r, y, copy):
        copy.wait_recv()

        def add(z, _):
            r[y, z] = g[y, z, ck] + r[y, z]
            return 0

        lax.fori_loop(0, 4, add, 0)

    def first_stage(r, ra, ss, qs):
        out = []
        for d in order:
            out.append(remote(r.at[off(cy, d), :, 0], ra.at[0, d - 1], ss.at[3 + d], qs.at[3 + d], at_y(d)))
            out.append(remote(r.at[:, off(cz, d), 1], ra.at[1, d - 1], ss.at[6 + d], qs.at[6 + d], at_z(d)))
        return out

    def first_sum(r, ra, copies):
        for cp in copies:
            cp.wait_recv()

        def add(n, _):
            for half, at in ((0, (cy, n)), (1, (n, cz))):
                total = r[at[0], at[1], half].astype(F32)
                for d in range(3):
                    total = total + ra[half, d, n].astype(F32)
                r[at[0], at[1], half] = total.astype(BF)
            return 0

        lax.fori_loop(0, 4, add, 0)

    def second_stage(r, rb, ss, qs):
        out = []
        for d in order:
            out.append(remote(r.at[cy, off(cz, d), 0], rb.at[0, d - 1], ss.at[9 + d], qs.at[9 + d], at_z(d)))
            out.append(remote(r.at[off(cy, d), cz, 1], rb.at[1, d - 1], ss.at[12 + d], qs.at[12 + d], at_y(d)))
        return out

    def second_sum(r, rb, copies):
        for cp in copies:
            cp.wait_recv()
        out = []
        for half in range(2):
            total = r[cy, cz, half].astype(F32)
            for d in range(3):
                total = total + rb[half, d].astype(F32)
            out.append(total)
        return out

    def weight_part(g, lhs, rhs, at, y):
        width = rhs.shape[1]
        part = dot(lhs[:, y * 256 : (y + 1) * 256], rhs[...], TN).astype(BF)
        g[y, :, :, :, :, at : at + width] = part.reshape(4, 2, 2, 16, width)

    core1 = []
    for y in range(4):
        weight_part(g1, post, gg, 0, y)
        weight_part(g1, post, ug, FF, y)
        core1.append(core_stage(g1, r1, s1, q1, y))

    ml_c = []
    for p in range(2):
        post_grad = collect_x(ppb, 0, p, post_c[p])
        back, term = row_norm_back(mid[piece(t, p), :], pg[...], post_grad)
        mgr[p * 32 : p * 32 + 32, :] = gy[piece(t, p), :].astype(F32) + back
        ml[piece(t, p), :] = mgr[p * 32 : p * 32 + 32, :].astype(BF)
        ml_c += spread_x(ml, 0, p)
        gain = jnp.sum(term, 0, keepdims=True)
        post_gain_term = gain if p == 0 else post_gain_term + gain

    for y in range(4):
        core_sum(g1, r1, y, core1[y])
    first1 = first_stage(r1, ra1, s1, q1)

    for y in range(4):
        weight_part(g3, gy, hid, 0, y)
    for cp in ml_c:
        cp.wait_recv()
    mlp_c = [[scatter_x(mpb, 1, p, d) for d in order] for p in range(2)]

    ag = dot(ml[...], wo_all[t], NT).astype(BF).astype(F32)
    for kv in range(2):
        to_diagonal(ag[:, kv * 128 : (kv + 1) * 128], kv, dobd)
    for s in range(2):
        for h in range(2):
            at = slice(h * 256, (h + 1) * 256)
            stats[s, 1:2, at] = jnp.sum(dobd[s, at, :].astype(F32).T * ot[s, h], 0, keepdims=True)
    dq[...] = jnp.zeros_like(dq)

    def back_step(j, s, kh, first, seen):
        at = slice(first, 512)
        kc, vc = chunk(0, j, s, kh), chunk(1, j, s, kh)
        q, do = qbd[s, at, :], dobd[s, at, :]
        p = jnp.exp(dot(kc, q, NT) - stats[s, 0:1, at])
        if seen is not None:
            p = jnp.where(seen, p, 0.0)
        ds = (p * (dot(vc, do, NT) - stats[s, 1:2, at])).astype(BF)
        where = pl.ds((s * 2 + kh) * 64, 64)
        dkv[j, :, :, 1, where, :] = dot(p.astype(BF), do).astype(BF).reshape(4, 2, 64, 128)
        dkv[j, :, :, 0, where, :] = dot(ds, q).astype(BF).reshape(4, 2, 64, 128)
        dq[s, at, :] += dot(ds, kc, TN)

    def key_core(j):
        return remote_copy(dkv.at[j, :, sib], r0.at[j], s0.at[j], q0.at[j], at_k)

    def key_along_y(j):
        d = lax.rem(j - cy + 4, 4)
        peer = ((j * 4 + cz) * 2 + ck, t)
        return remote_copy(r0.at[j, :, 0], ra0.at[0, d - 1], s0.at[3 + d], q0.at[3 + d], peer)

    def key_along_z(j):
        return [
            remote_copy(r0.at[j, off(cz, d), 1], ra0.at[1, d - 1, j], bs0.at[d - 1, j], bq0.at[d - 1, j], at_z(d))
            for d in order
        ]

    def key_step(n, _):
        j = off(cy, n + 1)

        @pl.when(n < 4)
        def _():
            @pl.when(j < cy)
            def _():
                for s in range(2):
                    back_step(j, s, 0, 0, None)
                    for kind in range(2):
                        dkv[j, :, :, kind, pl.ds((s * 2 + 1) * 64, 64), :] = jnp.zeros((4, 2, 64, 128), BF)

            @pl.when(j > cy)
            def _():
                for s in range(2):
                    back_step(j, s, 0, 256, None)
                    back_step(j, s, 1, 256, None)

            @pl.when(j == cy)
            def _():
                for s in range(2):
                    back_step(j, s, 0, 0, visible_front(512))
                    back_step(j, s, 1, 256, visible_back())

            key_core(j).start()

        @pl.when(n > 0)
        def _():
            done = off(cy, n)
            core_sum(dkv, r0, done, key_core(done))

            @pl.when(n < 4)
            def _():
                key_along_y(done).start()

            for cp in key_along_z(done):
                cp.start()

        return 0

    lax.fori_loop(0, 5, key_step, 0)
    first0 = []
    for y in range(4):
        sent.append(key_core(y))
        first0 += key_along_z(y)
    for d in order:
        first0.append(
            remote_copy(r0.at[off(cy, d), :, 0], ra0.at[0, d - 1], s0.at[3 + d], q0.at[3 + d], at_y(d))
        )
    sent.extend(first0)

    query_gain_term = jnp.zeros((1, 128), F32)
    for kv in range(2):
        parts = [
            from_diagonal(dq[s, h * 256 : (h + 1) * 256, :], kv) for s in range(2) for h in range(2)
        ]
        grads = rotate_back(jnp.concatenate(parts, 0) * 0.125)
        back, term = head_norm_back(qp[kv], query_gain, grads)
        dql[:, kv * 128 : (kv + 1) * 128] = back.astype(BF)
        query_gain_term = query_gain_term + jnp.sum(term, 0, keepdims=True)

    mixed_c = []
    for p in range(2):
        mixed_s[piece(t, p), :] = (mid[piece(t, p), :] + collect_x(mpb, 1, p, mlp_c[p])).astype(BF)
        mixed_c += spread_x(mixed_s, 1, p)

    first_sum(r0, ra0, first0)
    second0 = second_stage(r0, rb0, s0, q0)
    first_sum(r1, ra1, first1)
    second1 = second_stage(r1, rb1, s1, q1)

    core3 = []
    for y in range(4):
        weight_part(g3, ml, att_all.at[t], FF, y)
        weight_part(g3, nrm, dql, FF + 256, y)
        core3.append(core_stage(g3, r3, s3, q3, y))
    pp[...] = dot(dql[...], wq[...], NT)

    key_grad, value_grad = second_sum(r0, rb0, second0)
    back, term = head_norm_back(kp[...], key_gain, rotate_back(key_grad))
    kvl[:, 0:128] = back.astype(BF)
    kvl[:, 128:256] = value_grad.astype(BF)
    key_gain_term = jnp.sum(term, 0, keepdims=True)

    ipb[...] = (pp[...] + dot(kvl[:, 0:128], wk[...], NT) + dot(kvl[:, 128:256], wv[...], NT)).astype(BF)
    in_c = [[scatter_x(ipb, 2, p, d) for d in order] for p in range(2)]
    for y in range(4):
        core_sum(g3, r3, y, core3[y])
    first3 = first_stage(r3, ra3, s3, q3)
    for y in range(4):
        weight_part(g2, nrm, kvl, 0, y)
    core2 = [core_stage(g2, r2, s2, q2, y) for y in range(4)]

    for half, total in enumerate(second_sum(r1, rb1, second1)):
        rows = slice(half * 16, half * 16 + 16)
        gate_out[rows, :] = total[:, 0:FF]
        up_out[rows, :] = total[:, FF : 2 * FF]
    for y in range(4):
        core_sum(g2, r2, y, core2[y])
    first2 = first_stage(r2, ra2, s2, q2)

    bases = (0, 3, 10)

    def gain_stage(n, peers):
        return [
            remote(gv.at[n], gr.at[bases[n] + i], gss.at[bases[n] + i], grs.at[bases[n] + i], peer)
            for i, peer in enumerate(peers)
        ]

    def gain_sum(n, copies):
        whole = gv[n]
        for i, cp in enumerate(copies):
            cp.wait_recv()
            whole = whole + gr[bases[n] + i]
        return whole

    gv[0, 1:2, :] = post_gain_term
    gv[0, 2:8, :] = jnp.zeros((6, 1024), F32)
    gv[0, 2:3, 0:128] = query_gain_term + pltpu.roll(query_gain_term, 64, 1)
    gv[0, 3:4, 0:128] = key_gain_term + pltpu.roll(key_gain_term, 64, 1)
    xg_c = []
    for p in range(2):
        back, term = row_norm_back(
            x[piece(t, p), :].astype(F32), ng[...], collect_x(ipb, 2, p, in_c[p])
        )
        gain = jnp.sum(term, 0, keepdims=True)
        xg_s[piece(t, p), :] = (mgr[p * 32 : p * 32 + 32, :] + back).astype(BF)
        if p == 0:
            norm_gain_term = gain
        else:
            gv[0, 0:1, :] = norm_gain_term + gain
            gain_c = gain_stage(0, [at_x(d) for d in order])
        xg_c += spread_x(xg_s, 2, p)
    gv[1] = gain_sum(0, gain_c)
    gain_c = gain_stage(1, [at_k] + [at_y(d) for d in order] + [at_ky(d) for d in order])
    first_sum(r2, ra2, first2)
    second2 = second_stage(r2, rb2, s2, q2)
    first_sum(r3, ra3, first3)
    second3 = second_stage(r3, rb3, s3, q3)
    gv[2] = gain_sum(1, gain_c)
    gain_c = gain_stage(2, [at_z(d) for d in order])
    for cp in mixed_c:
        cp.wait_recv()
    mixed_out[...] = mixed_s[...]
    for half, total in enumerate(second_sum(r3, rb3, second3)):
        rows = slice(half * 16, half * 16 + 16)
        down_out[rows, :] = total[:, 0:FF]
        wo_out[rows, :] = total[:, FF : FF + 256]
        wq_out[rows, :] = total[:, FF + 256 : FF + 512]
    for half, total in enumerate(second_sum(r2, rb2, second2)):
        rows = slice(half * 16, half * 16 + 16)
        wk_out[rows, :] = total[:, 0:128]
        wv_out[rows, :] = total[:, 128:256]
    gains = gain_sum(2, gain_c)
    for cp in xg_c:
        cp.wait_recv()
    xgrad_out[...] = xg_s[...]
    ng_out[...] = gains[0:1, :]
    pg_out[...] = gains[1:2, :]
    qg_out[...] = gains[2:3, 0:64]
    kg_out[...] = gains[3:4, 0:64]
    for cp in sent:
        cp.wait_send()


def hand_out(*refs):
    count = len(refs) // 2
    for source, target in zip(refs[:count], refs[count:]):
        target[...] = source[...]


def on_device(
    tokens, norm_gain, query_weight, key_weight, value_weight, query_gain, key_gain, out_weight,
    post_gain, gate_weight, up_weight, down_weight, cotangent,
):
    x = tokens.reshape(256, 1024)
    gy = cotangent.reshape(256, 1024)
    tables = [jnp.asarray(a) for a in rope_constants()]
    cr, sr, cb, sb = tables
    vm = pl.BlockSpec(memory_space=pltpu.VMEM)
    hbm = pl.BlockSpec(memory_space=pl.ANY)
    V = pltpu.VMEM
    sem = lambda *s: pltpu.SemaphoreType.DMA(s)

    def ring(rows, width):
        return [V(lead + (rows, width), BF) for lead in ((4, 4, 2, 2), (4, 4, 2), (2, 3, 4), (2, 3))]

    scratch = [
        V((1024, FF), BF), V((1024, FF), BF), V((FF, 1024), BF),
        V((1024, 256), BF), V((256, 1024), BF), V((4, 256, 1024), BF),
        V((256, 1024), BF), V((2, 32, 256, 128), BF), V((256, 128), F32), V((2, 256, 128), F32),
        V((256, 128), F32), V((256, 128), F32), V((2, 512, 128), BF), V((2, 512, 128), BF),
        V((2, 2, 128, 256), F32), V((2, 2, 8, 256), F32), V((2, 8, 512), F32), V((4, 256, 256), BF),
        V((256, 1024), F32), V((256, 1024), BF), V((256, FF), BF), V((256, FF), BF), V((256, FF), BF),
        V((256, 1024), F32), V((256, 1024), BF), V((256, 1024), BF), V((256, 1024), BF),
        V((3, 3, 64, 1024), BF),
        V((256, 1024), BF), V((64, 1024), F32), V((256, 1024), BF), V((256, 1024), BF),
        V((2, 512, 128), F32), V((256, 256), BF), V((256, 256), BF),
        *ring(16, G1X),
        *ring(256, 128),
        *ring(16, G2X),
        *ring(16, G3X),
        V((3, 8, 1024), F32), V((13, 8, 1024), F32),
        sem(6), sem(2, 32), sem(2, 32), sem(9, 3), sem(9, 3), sem(6, 3), sem(6, 3), sem(3), sem(3),
        *[sem(16)] * 8, sem(3, 4), sem(3, 4), sem(13), sem(13),
    ]
    shape = jax.ShapeDtypeStruct
    outs = [
        shape((256, 1024), BF), shape((256, 1024), BF), shape((1, 1024), F32),
        shape((32, 256), F32), shape((32, 128), F32), shape((32, 128), F32),
        shape((1, 64), F32), shape((1, 64), F32), shape((32, 256), F32), shape((1, 1024), F32),
        shape((32, FF), F32), shape((32, FF), F32), shape((32, FF), F32),
    ]
    results = pl.pallas_call(
        kernel,
        name="block",
        out_shape=outs,
        in_specs=[vm] * 2 + [hbm] + [vm] * 4 + [hbm] + [vm] + [hbm] * 4 + [vm] * 4,
        out_specs=[vm] * 13,
        scratch_shapes=scratch,
        compiler_params=pltpu.CompilerParams(
            collective_id=0, has_side_effects=True, vmem_limit_bytes=63 * 2**20
        ),
    )(
        x, norm_gain.reshape(1, 1024), query_weight, key_weight, value_weight,
        query_gain.reshape(1, 64), key_gain.reshape(1, 64),
        out_weight, post_gain.reshape(1, 1024), gate_weight, up_weight, down_weight, gy, cr, sr, cb, sb,
    )
    results = pl.pallas_call(
        hand_out,
        name="hand_out",
        out_shape=outs,
        in_specs=[vm] * 13,
        out_specs=[vm] * 13,
    )(*results)
    mixed, xgrad, ng, wq, wk, wv, qg, kg, wo, pg, gate, up, down = results
    place = (2, 2, 1, 64, 1024)
    return (
        mixed.reshape(place), xgrad.reshape(place), ng.reshape(1024), wq, wk, wv, qg.reshape(64), kg.reshape(64),
        wo.T, pg.reshape(1024), gate, up, down.T,
    )


def solution(mesh):
    tok = P(None, None, "ctx", None, None)
    col = P(None, "tp")
    row = P("tp", None)
    return jax.shard_map(
        on_device,
        mesh=mesh,
        in_specs=(tok, P(), col, col, col, P(), P(), row, P(), col, col, row, tok),
        out_specs=(
            tok, tok, P(), P("ctx", "tp"), P("ctx", "tp"), P("ctx", "tp"), P(), P(), P("tp", "ctx"), P(),
            P("ctx", "tp"), P("ctx", "tp"), P("tp", "ctx"),
        ),
        check_vma=False,
    )
```
